32 devices in a mesh: dp: 2 (over y), expert: 16 (over z, x, core).
Axes of the slice: x: 2, y: 2, z: 4, core: 2. Of those that a mesh axis runs over, the one named last changes fastest.
Arguments:
- tokens: bfloat16 [4096, 3584], P(('dp', 'expert')), may hold values from -6 to 6
- out_cotangent: bfloat16 [4096, 3584], P(('dp', 'expert')), may hold values from -6 to 6
- expert_ids: int32 [4096, 8], P(('dp', 'expert')), may hold values from 0 to 255, as said below
- gate_fixed: int32 [4096, 8], P(('dp', 'expert')), may hold values from 4096 to 65535
- w_gate: bfloat16 [16, 3584, 128], P('expert', 'dp'), may hold values from -0.09375 to 0.09375
- w_up: bfloat16 [16, 3584, 128], P('expert', 'dp'), may hold values from -0.09375 to 0.09375
- w_down: bfloat16 [16, 3584, 128], P('expert', 'dp'), may hold values from -0.125 to 0.125
Outputs:
- layer_out: bfloat16 [4096, 3584], P(('dp', 'expert'))
- token_grad: bfloat16 [4096, 3584], P(('dp', 'expert'))
- grad_gate: float32 [16, 3584, 128], P('expert', 'dp')
- grad_up: float32 [16, 3584, 128], P('expert', 'dp')
- grad_down: float32 [16, 3584, 128], P('expert', 'dp')
The draws below stay inside these ranges and needn't reach their ends.
Inputs may be any that keep to these rules, and one draw needn't show every extreme that they name: `expert_ids`: each row names 8 different experts. Within the 128 rows of one device each expert below 1 is named by 1 to 4 rows; in every draw one expert below 1 is named by exactly 4 rows on every device.
All inputs are finite; a program needn't handle non-finite values.
Results may differ from the reference program's by a relative error of at most 0.014.
Values may be sent and summed in bfloat16 or wider, within the bound.
A program may use at most 128 MiB of HBM per device.

```python
import jax
import jax.numpy as jnp
from jax import lax

D = 3584
HIDDEN_SIZE = 2048
EXPERTS_ALL = 256
TOP = 8
SPLIT = 16
CAP = 4
TOK_DEV = 128
HID_DEV = 128
EXP_WIN = 1
SHARDS = 16
TOKENS = 4096
N_DP = 2


def draw_expert_ids(key, part):
    blocks = TOKENS // TOK_DEV
    others_count = EXPERTS_ALL - EXP_WIN
    keys = jax.random.split(jax.random.fold_in(key, 7), 5)
    counts = jax.random.randint(keys[0], (blocks, EXP_WIN), 1, CAP + 1)
    hot = jax.random.randint(keys[1], (), 0, EXP_WIN)
    column = jnp.arange(EXP_WIN, dtype=jnp.int32)
    counts = jnp.where(column[None, :] == hot, CAP, counts)
    scores = jax.random.randint(keys[2], (blocks, EXP_WIN, TOK_DEV), 0, 1 << 20) * TOK_DEV
    scores = scores + jnp.arange(TOK_DEV, dtype=jnp.int32)[None, None, :]
    ranks = jnp.argsort(jnp.argsort(scores, axis=-1), axis=-1)
    member = ranks < counts[:, :, None]
    member = jnp.transpose(member, (0, 2, 1)).reshape(TOKENS, EXP_WIN)
    other_scores = jax.random.randint(keys[3], (TOKENS, others_count), 0, 1 << 20) * 256
    other_scores = other_scores + jnp.arange(others_count, dtype=jnp.int32)[None, :]
    unused, others = lax.top_k(other_scores, TOP)
    others = others.astype(jnp.int32) + EXP_WIN
    running = jnp.cumsum(member.astype(jnp.int32), axis=1)
    total = running[:, -1:]
    slots = jnp.arange(TOP, dtype=jnp.int32)
    match = jnp.logical_and(member[:, :, None], running[:, :, None] == slots[None, None, :] + 1)
    win_id = jnp.sum(jnp.where(match, column[None, :, None], 0), axis=1)
    index = jnp.clip(slots[None, :] - total, 0, TOP - 1)
    other_id = jnp.take_along_axis(others, index, axis=1)
    chosen = jnp.where(slots[None, :] < total, win_id, other_id)
    order_scores = jax.random.randint(keys[4], (TOKENS, TOP), 0, 1 << 20) * TOP + slots[None, :]
    order = jnp.argsort(order_scores, axis=1)
    return jnp.take_along_axis(chosen, order, axis=1).astype(jnp.int32)


def set_ends(drawn, key, smallest, top_value):
    dims = drawn.shape
    index_at = [jax.random.randint(jax.random.fold_in(key, axis), (), 0, dims[axis]) for axis in range(len(dims))]
    drawn = drawn.at[tuple(index_at)].set(smallest)
    longest = dims.index(max(dims))
    index_at[longest] = (index_at[longest] + 1) % dims[longest]
    return drawn.at[tuple(index_at)].set(top_value)


def shard_levels(stream_key, dims, cuts, low, top_value):
    def one(axis_at, shards_of):
        steps = jax.random.uniform(jax.random.fold_in(jax.random.fold_in(stream_key, 6), axis_at), (shards_of,), jnp.float32, low / len(cuts), top_value / len(cuts))
        return jnp.repeat(jnp.exp(steps), dims[axis_at] // shards_of).reshape((-1,) + (1,) * (len(dims) - axis_at - 1))

    factor_of = one(*cuts[0])
    for cut in cuts[1:]:
        factor_of = factor_of * one(*cut)
    return factor_of


def scatter_about(rng, extent, width, most, cuts=(), kind=jnp.bfloat16):
    array = width * jax.random.normal(rng, extent, jnp.float32)
    if cuts:
        array = array * shard_levels(rng, extent, cuts, -0.22, 0.18)
    return jnp.clip(array, -most, most).astype(kind)


def setup_inputs(seed: int = 0) -> dict:
    key_list = jax.random.split(jax.random.key(seed), 8)
    tokens = scatter_about(key_list[0], (TOKENS, D), 1.0, 6.0, ((0, 32),))
    out_cotangent = scatter_about(key_list[1], (TOKENS, D), 1.0, 6.0, ((0, 32),))
    expert_ids = draw_expert_ids(jax.random.fold_in(key_list[7], 71), 0)
    gate_fixed = set_ends(jax.random.randint(key_list[3], (TOKENS, TOP), 4096, 65536), jax.random.fold_in(key_list[3], 1), 4096, 65535).astype(jnp.int32)
    w_gate = scatter_about(key_list[4], (SHARDS, D, HID_DEV), D ** -0.5, 0.09375, ((0, 16), (1, 2)))
    w_up = scatter_about(key_list[5], (SHARDS, D, HID_DEV), D ** -0.5, 0.09375, ((0, 16), (1, 2)))
    w_down = scatter_about(key_list[6], (SHARDS, D, HID_DEV), HIDDEN_SIZE ** -0.5, 0.125, ((0, 16), (1, 2)))
    return {"tokens": tokens, "out_cotangent": out_cotangent, "expert_ids": expert_ids, "gate_fixed": gate_fixed, "w_gate": w_gate, "w_up": w_up, "w_down": w_down}


SCALE = 2.0 ** -16
HIGH = lax.Precision.HIGHEST


def routing(ids, gates):
    wanted = jnp.arange(EXP_WIN, dtype=jnp.int32)
    hits = ids[:, :, None] == wanted[None, None, :]
    member = jnp.any(hits, axis=1)
    weight = jnp.sum(jnp.where(hits, gates[:, :, None], 0), axis=1).astype(jnp.float32) * SCALE
    rank = jnp.cumsum(member.astype(jnp.int32), axis=0) - 1
    slots = jnp.arange(CAP, dtype=jnp.int32)
    pick = jnp.logical_and(member[:, :, None], rank[:, :, None] == slots[None, None, :])
    select = jnp.where(pick, 1.0, 0.0).astype(jnp.float32)
    slot_gate = jnp.sum(select * weight[:, :, None], axis=0)
    return select, slot_gate


def expert_weights(shards):
    full = shards.reshape(EXP_WIN, SPLIT, D, HID_DEV).transpose(0, 2, 1, 3)
    return full.reshape(EXP_WIN, D, HIDDEN_SIZE)


def shard_layout(grads):
    return grads.reshape(EXP_WIN, D, SPLIT, HID_DEV).transpose(0, 2, 1, 3).reshape(EXP_WIN * SPLIT, D, HID_DEV)


def reference(tokens, out_cotangent, expert_ids, gate_fixed, w_gate, w_up, w_down):
    blocks = TOKENS // TOK_DEV
    tok3 = tokens.reshape(blocks, TOK_DEV, D).astype(jnp.float32)
    cot3 = out_cotangent.reshape(blocks, TOK_DEV, D).astype(jnp.float32)
    select, slot_gate = jax.vmap(routing)(expert_ids.reshape(blocks, TOK_DEV, TOP),
                                          gate_fixed.reshape(blocks, TOK_DEV, TOP))
    slot_tokens = jnp.einsum('btec,btd->ebcd', select, tok3, precision=HIGH).astype(jnp.bfloat16)
    picked = jnp.einsum('btec,btd->ebcd', select, cot3, precision=HIGH)
    slot_cot = (jnp.transpose(slot_gate, (1, 0, 2))[:, :, :, None] * picked).astype(jnp.bfloat16)
    wg_all = expert_weights(w_gate)
    wu_all = expert_weights(w_up)
    wd_all = expert_weights(w_down)

    def one_expert(items):
        xs, dos, wg, wu, wd = items
        rows = xs.reshape(blocks * CAP, D)
        drows = dos.reshape(blocks * CAP, D)
        gate_pre = jnp.dot(rows, wg, preferred_element_type=jnp.float32)
        up_pre = jnp.dot(rows, wu, preferred_element_type=jnp.float32)
        sig = jax.nn.sigmoid(gate_pre)
        act = gate_pre * sig
        hidden = (act * up_pre).astype(jnp.bfloat16)
        expert_out = jnp.dot(hidden, wd.T, preferred_element_type=jnp.float32).astype(jnp.bfloat16)
        d_hidden = jnp.dot(drows, wd, preferred_element_type=jnp.float32)
        d_gate = (d_hidden * up_pre * sig * (1.0 + gate_pre * (1.0 - sig))).astype(jnp.bfloat16)
        d_up = (d_hidden * act).astype(jnp.bfloat16)
        slot_grad = (jnp.dot(d_gate, wg.T, preferred_element_type=jnp.float32)
                     + jnp.dot(d_up, wu.T, preferred_element_type=jnp.float32)).astype(jnp.bfloat16)
        xpart = rows.reshape(N_DP, -1, D).astype(jnp.float32)
        dpart = drows.reshape(N_DP, -1, D).astype(jnp.float32)

        def partial_sum(left, right):
            terms = jnp.einsum('prd,prh->pdh', left, right.reshape(N_DP, -1, HIDDEN_SIZE).astype(jnp.float32), precision=HIGH)
            return jnp.sum(terms.astype(jnp.bfloat16).astype(jnp.float32), axis=0)

        grad_g = partial_sum(xpart, d_gate)
        grad_u = partial_sum(xpart, d_up)
        grad_d = partial_sum(dpart, hidden)
        return (expert_out.reshape(blocks, CAP, D), slot_grad.reshape(blocks, CAP, D), grad_g, grad_u, grad_d)

    outs, grads, grad_g, grad_u, grad_d = lax.map(one_expert, (slot_tokens, slot_cot, wg_all, wu_all, wd_all))
    weighted = select * slot_gate[:, None, :, :]
    layer_out = jnp.einsum('btec,ebcd->btd', weighted, outs.astype(jnp.float32), precision=HIGH)
    token_grad = jnp.einsum('btec,ebcd->btd', select, grads.astype(jnp.float32), precision=HIGH)
    return (layer_out.astype(jnp.bfloat16).reshape(TOKENS, D),
            token_grad.astype(jnp.bfloat16).reshape(TOKENS, D),
            shard_layout(grad_g), shard_layout(grad_u), shard_layout(grad_d))
```

```python
import jax
import jax.numpy as jnp
from jax import lax
from jax.sharding import PartitionSpec as P
from jax.experimental import pallas as pl
from jax.experimental.pallas import tpu as pltpu

SPLIT = 16
CAP = 4


SCALE = 2.0 ** (-16)
HIGH = lax.Precision.HIGHEST


def routing(ids, gates, window, capacity):
    wanted = jnp.arange(window, dtype=jnp.int32)
    hits = ids[:, :, None] == wanted[None, None, :]
    member = jnp.any(hits, axis=1)
    weight = jnp.sum(jnp.where(hits, gates[:, :, None], 0), axis=1).astype(jnp.float32) * SCALE
    rank = jnp.cumsum(member.astype(jnp.int32), axis=0) - 1
    slots = jnp.arange(capacity, dtype=jnp.int32)
    pick = jnp.logical_and(member[:, :, None], rank[:, :, None] == slots[None, None, :])
    select = jnp.where(pick, 1.0, 0.0).astype(jnp.float32)
    slot_gate = jnp.sum(select * weight[:, :, None], axis=0)
    return (select, slot_gate)


def expert_math(inputs, cotangents, gate_w, up_w, down_w):
    gate_pre = jnp.einsum("prf,pfh->rh", inputs, gate_w, preferred_element_type=jnp.float32)
    up_pre = jnp.einsum("prf,pfh->rh", inputs, up_w, preferred_element_type=jnp.float32)
    sig = jax.nn.sigmoid(gate_pre)
    act = gate_pre * sig
    hidden = (act * up_pre).astype(jnp.bfloat16)
    partial_out = jnp.einsum("rh,pfh->prf", hidden, down_w, preferred_element_type=jnp.float32)
    d_hidden = jnp.einsum("prf,pfh->rh", cotangents, down_w, preferred_element_type=jnp.float32)
    d_gate = (d_hidden * up_pre * sig * (1.0 + gate_pre * (1.0 - sig))).astype(jnp.bfloat16)
    d_up = (d_hidden * act).astype(jnp.bfloat16)
    partial_grad = jnp.einsum(
        "rh,pfh->prf", d_gate, gate_w, preferred_element_type=jnp.float32
    ) + jnp.einsum("rh,pfh->prf", d_up, up_w, preferred_element_type=jnp.float32)
    term = jnp.concatenate(
        [
            jnp.einsum("prf,rh->pfh", inputs, d_gate, preferred_element_type=jnp.float32),
            jnp.einsum("prf,rh->pfh", inputs, d_up, preferred_element_type=jnp.float32),
            jnp.einsum("prf,rh->pfh", cotangents, hidden, preferred_element_type=jnp.float32),
        ],
        axis=2,
    )
    return (partial_out, partial_grad, term.reshape(-1, term.shape[2]))


def per_device(tokens, out_cotangent, expert_ids, gate_fixed, w_gate, w_up, w_down):
    tok_rows, width = tokens.shape
    groups = lax.axis_size("expert")
    window = groups // SPLIT
    hid = w_gate.shape[2]
    parts = 1
    feat = width // parts
    select, slot_gate = routing(expert_ids, gate_fixed, window, CAP)
    select_b = select.astype(jnp.bfloat16)
    tok3 = tokens.reshape(tok_rows, parts, feat)
    cot3 = out_cotangent.reshape(tok_rows, parts, feat)
    slot_tokens = jnp.einsum(
        "tec,tsf->escf", select_b, tok3, preferred_element_type=jnp.float32
    ).astype(jnp.bfloat16)
    picked = jnp.einsum("tec,tsf->escf", select_b, cot3, preferred_element_type=jnp.float32)
    slot_cot = (picked * slot_gate[:, None, :, None]).astype(jnp.bfloat16)
    payload = jnp.stack([slot_tokens, slot_cot], axis=2)
    gate_full, up_full, down_full = (
        lax.all_gather(w_gate, "dp", axis=1, tiled=True),
        lax.all_gather(w_up, "dp", axis=1, tiled=True),
        lax.all_gather(w_down, "dp", axis=1, tiled=True),
    )
    outgoing = jnp.broadcast_to(payload, (window, SPLIT, 2, CAP, width)).reshape(
        groups, 2, CAP, width
    )
    arrived = lax.all_to_all(outgoing, "expert", split_axis=0, concat_axis=0, tiled=True)
    pieces = arrived[None]
    inputs = pieces[:, :, 0].reshape(parts, groups * CAP, feat)
    cotangents = pieces[:, :, 1].reshape(parts, groups * CAP, feat)
    partial_out, partial_grad, term = expert_math(inputs, cotangents, gate_full, up_full, down_full)
    summed = lax.psum_scatter(
        term.astype(jnp.bfloat16), "dp", scatter_dimension=0, tiled=True
    ).astype(jnp.float32)
    grad_gate = summed[:, :hid][None]
    grad_up = summed[:, hid : 2 * hid][None]
    grad_down = summed[:, 2 * hid :][None]
    results = jnp.stack(
        [
            partial_out.reshape(parts, groups, CAP, feat),
            partial_grad.reshape(parts, groups, CAP, feat),
        ],
        axis=2,
    )
    returned = lax.all_to_all(
        results[0].astype(jnp.bfloat16), "expert", split_axis=0, concat_axis=0, tiled=True
    ).astype(jnp.float32)
    combined = jnp.sum(
        returned.reshape(window, SPLIT, 2, CAP, width), axis=1, keepdims=True
    ).astype(jnp.bfloat16)
    weighted = select * slot_gate[None, :, :]
    layer_out = jnp.einsum(
        "tec,ehcf->thf", weighted, combined[:, :, 0].astype(jnp.float32), precision=HIGH
    )
    token_grad = jnp.einsum(
        "tec,ehcf->thf", select, combined[:, :, 1].astype(jnp.float32), precision=HIGH
    )
    return (
        layer_out.reshape(tok_rows, width).astype(jnp.bfloat16),
        token_grad.reshape(tok_rows, width).astype(jnp.bfloat16),
        grad_gate,
        grad_up,
        grad_down,
    )


MESH = pl.DeviceIdType.MESH
F32 = jnp.float32
BF16 = jnp.bfloat16


def row_ids(shape):
    return lax.broadcasted_iota(jnp.int32, shape, 0)


def fold(v):
    half = v.shape[1] // 2
    return jnp.concatenate([v[:, :half], v[:, half:]], axis=0)


def unfold(v):
    rows = v.shape[0] // 2
    return jnp.concatenate([v[:rows], v[rows:]], axis=1)


def exchange_kernel(
    ids_ref, gates_ref, tok_hbm, cot_hbm, wg_hbm, wu_hbm, wd_hbm,
    x_out, act_out, slot_out, sel_out,
    tok_v, cot_v, w_v, gath, act_v, part, pex_s, pex_r, res, ra, sb, rb, sc, rc,
    ys, yr, ys2, yr2, load_sem, send_sem, recv_sem,
):
    y = lax.axis_index("dp")
    e = lax.axis_index("expert")
    z, x, c = e // 4, (e // 2) % 2, e % 2

    def dev(zz, xx, cc):
        return zz * 4 + xx * 2 + cc

    def pos(zz, xx, cc):
        return cc * 8 + xx * 4 + zz

    near = [z, z + 1 - 2 * (z % 2), (z + 2) % 4, 3 - z]
    peer_y = (1 - y, e)
    peer_c = (y, dev(z, x, 1 - c))
    peer_x = (y, dev(z, 1 - x, c))
    peer_z = [None] + [(y, dev(zz, x, c)) for zz in near[1:]]

    started = []

    def remote(src, dst, target):
        n = len(started)
        copy = pltpu.make_async_remote_copy(
            src_ref=src, dst_ref=dst, send_sem=send_sem.at[n], recv_sem=recv_sem.at[n],
            device_id=target, device_id_type=MESH,
        )
        copy.start()
        started.append(copy)
        return copy

    loads = [
        pltpu.make_async_copy(tok_hbm, tok_v, load_sem.at[0]),
        pltpu.make_async_copy(cot_hbm, cot_v, load_sem.at[1]),
        pltpu.make_async_copy(wg_hbm, w_v.at[:, 0:128], load_sem.at[2]),
        pltpu.make_async_copy(wu_hbm, w_v.at[:, 128:256], load_sem.at[3]),
        pltpu.make_async_copy(wd_hbm, w_v.at[:, 256:384], load_sem.at[4]),
    ]
    for load in loads:
        load.start()
    barrier = pltpu.get_barrier_semaphore()
    greeted = [peer_y, peer_c, peer_x] + peer_z[1:]
    for target in greeted:
        pl.semaphore_signal(barrier, inc=1, device_id=target, device_id_type=MESH)

    hits = ids_ref[...] == 0
    member = jnp.sum(jnp.where(hits, 1.0, 0.0), axis=1, keepdims=True)
    weight = jnp.sum(jnp.where(hits, gates_ref[...].astype(F32), 0.0), axis=1, keepdims=True) * SCALE
    n_tok = member.shape[0]
    square = (n_tok, n_tok)
    lane = lax.broadcasted_iota(jnp.int32, square, 1)
    earlier = jnp.where(lane < row_ids(square), 1.0, 0.0).astype(BF16)
    spread = jnp.broadcast_to(member, square)
    rank = jnp.dot(earlier, spread.astype(BF16), preferred_element_type=F32)
    wanted = jnp.where(lane < 2 * CAP, lane % CAP, n_tok).astype(F32)
    sel = jnp.where(jnp.logical_and(rank == wanted, spread > 0.5), 1.0, 0.0)
    sel_out[...] = sel.astype(BF16)
    sel_t = jnp.transpose(sel)[:8].astype(BF16)
    gate8 = jnp.sum(jnp.transpose(sel * weight)[:8], axis=1, keepdims=True)

    loads[0].wait()
    tok8 = jnp.dot(sel_t, tok_v[...], preferred_element_type=F32)
    loads[1].wait()
    cot8 = jnp.dot(sel_t, cot_v[...], preferred_element_type=F32) * gate8
    half = tok8.shape[1] // 2
    low = row_ids((8, half)) < 4

    def mine(v, flip=False):
        first, second = v[:, :half], v[:, half:]
        return jnp.where((y == 0) != flip, first, second)

    ys[...] = fold(jnp.where(low, mine(tok8, True), mine(cot8, True))).astype(BF16)
    pl.semaphore_wait(barrier, len(greeted))
    swap = remote(ys, yr, peer_y)
    own_tok, own_cot = mine(tok8), mine(cot8)
    swap.wait_recv()
    got = unfold(yr[...].astype(F32))
    got_r = pltpu.roll(got, 4, 0)
    own_rows = jnp.logical_xor(low, y != 0)
    chunk = jnp.concatenate(
        [
            jnp.where(own_rows, own_tok, jnp.where(low, got, got_r)),
            jnp.where(own_rows, own_cot, jnp.where(low, got_r, got)),
        ],
        axis=0,
    )
    here = pos(z, x, c)
    gath[here] = chunk.astype(BF16)

    over_z, over_x, over_c = [None], [], []
    for k in (1, 2, 3):
        over_z.append(remote(gath.at[here], gath.at[here], peer_z[k]))
    for k in range(4):
        at = pos(near[k], x, c)
        if k:
            over_z[k].wait_recv()
        over_x.append(remote(gath.at[at], gath.at[at], peer_x))
        over_c.append(remote(gath.at[at], gath.at[at], peer_c))
    for k in range(4):
        at = pos(near[k], 1 - x, c)
        over_x[k].wait_recv()
        over_c.append(remote(gath.at[at], gath.at[at], peer_c))

    for load in loads[2:]:
        load.wait()

    def project(h):
        rows = gath[pl.ds(h * 8, 8)].reshape(128, half)
        p = jnp.dot(rows, w_v[...], preferred_element_type=F32).reshape(8, 16, 384)
        both = jnp.concatenate([p[:, :8, :256], p[:, 8:, 256:]], axis=2).reshape(64, 384)
        part[h] = both
        pex_s[h] = both.astype(BF16)
        return remote(pex_s.at[h], pex_r.at[h], peer_y)

    def activate(h):
        total = part[h] + pex_r[h].astype(F32)
        gate_pre, up_pre, d_hidden = total[:, :128], total[:, 128:256], total[:, 256:]
        sig = jax.nn.sigmoid(gate_pre)
        act = gate_pre * sig
        hidden = (act * up_pre).astype(BF16)
        d_gate = (d_hidden * up_pre * sig * (1.0 + gate_pre * (1.0 - sig))).astype(BF16)
        d_up = (d_hidden * act).astype(BF16)
        d_both = jnp.concatenate([d_gate, d_up], axis=1)
        nt = (((1,), (1,)), ((), ()))
        out = lax.dot_general(hidden, w_v[:, 256:], nt, preferred_element_type=F32)
        grad = lax.dot_general(d_both, w_v[:, :256], nt, preferred_element_type=F32)
        res[pl.ds(h * 8, 8)] = jnp.concatenate(
            [out.reshape(8, 8, half), grad.reshape(8, 8, half)], axis=1
        ).astype(BF16)
        top = jnp.concatenate([d_both.astype(F32).reshape(8, 8, 256), jnp.zeros((8, 8, 128), F32)], axis=2)
        bottom = jnp.concatenate([jnp.zeros((8, 8, 256), F32), hidden.astype(F32).reshape(8, 8, 128)], axis=2)
        act_v[pl.ds(h * 8, 8)] = jnp.concatenate([top, bottom], axis=1).astype(BF16)

    swap_own = project(c)
    for copy in over_c:
        copy.wait_recv()
    swap_other = project(1 - c)
    keep_x = pltpu.make_async_copy(gath, x_out, load_sem.at[5])
    keep_x.start()
    swap_other.wait_recv()
    activate(1 - c)
    to_core = []
    for xx in (1 - x, x):
        src = res.at[pl.ds((1 - c) * 8 + xx * 4, 4)]
        to_core.append(remote(src, ra.at[pl.ds(xx * 4, 4)], peer_c))
    swap_own.wait_recv()
    activate(c)
    keep_act = pltpu.make_async_copy(act_v, act_out, load_sem.at[6])
    keep_act.start()
    to_core[0].wait_recv()
    to_x = [None] * 4
    for k in (3, 2, 1, 0):
        zz = near[k]
        sb[k] = (res[pos(zz, 1 - x, c)].astype(F32) + ra[(1 - x) * 4 + zz].astype(F32)).astype(BF16)
        to_x[k] = remote(sb.at[k], rb.at[k], peer_x)
    to_core[1].wait_recv()

    def summed(k):
        zz = near[k]
        mid = res[pos(zz, x, c)].astype(F32) + ra[x * 4 + zz].astype(F32)
        to_x[k].wait_recv()
        return mid + rb[k].astype(F32)

    to_z = [None] * 4
    for k in (3, 2, 1):
        sc[k] = summed(k).astype(BF16)
        to_z[k] = remote(sc.at[k], rc.at[k], peer_z[k])
    total = summed(0)
    for k in (1, 2, 3):
        to_z[k].wait_recv()
        total = total + rc[k].astype(F32)
    out8, grad8 = total[:8], total[8:]
    for_0 = jnp.where(low, out8, pltpu.roll(grad8, 4, 0))
    for_1 = jnp.where(low, pltpu.roll(out8, 4, 0), grad8)
    ys2[...] = fold(jnp.where(y == 0, for_1, for_0)).astype(BF16)
    swap = remote(ys2, yr2, peer_y)
    mine8 = jnp.where(y == 0, for_0, for_1).astype(BF16).astype(F32)
    scale = jnp.where(row_ids((8, 1)) < 4, gate8, 1.0)
    swap.wait_recv()
    got = unfold(yr2[...].astype(F32))
    slot_out[:, :half] = jnp.where(y == 0, mine8, got) * scale
    slot_out[:, half:] = jnp.where(y == 0, got, mine8) * scale
    keep_x.wait()
    keep_act.wait()
    for copy in started:
        copy.wait_send()


def output_kernel(x_ref, act_ref, slot_ref, sel_ref, out_ref, tg_ref, gg_ref, gu_ref, gd_ref):
    sel = sel_ref[...][:, :8].astype(F32)
    lane = lax.broadcasted_iota(jnp.int32, sel.shape, 1)
    slots = slot_ref[...].astype(BF16)
    for ref, keep in ((out_ref, lane < 4), (tg_ref, lane >= 4)):
        picks = jnp.where(keep, sel, 0.0).astype(BF16)
        ref[...] = jnp.dot(picks, slots, preferred_element_type=F32).astype(BF16)
    tn = (((0,), (0,)), ((), ()))
    grads = lax.dot_general(x_ref[...], act_ref[...], tn, preferred_element_type=F32)
    for n, ref in enumerate((gg_ref, gu_ref, gd_ref)):
        ref[...] = grads[:, n * 128 : (n + 1) * 128]


def per_device_fused(tokens, out_cotangent, expert_ids, gate_fixed, w_gate, w_up, w_down):
    n_tok, width = tokens.shape
    half = width // 2
    hbm = pl.BlockSpec(memory_space=pl.ANY)
    vmem = pl.BlockSpec(memory_space=pltpu.VMEM)
    copies = 28
    chunks = lambda n: pltpu.VMEM((n, 16, half), BF16)
    x_all, act, slots, sel = pl.pallas_call(
        exchange_kernel,
        out_shape=(
            jax.ShapeDtypeStruct((16, 16, half), BF16),
            jax.ShapeDtypeStruct((16, 16, 384), BF16),
            jax.ShapeDtypeStruct((8, width), F32),
            jax.ShapeDtypeStruct((n_tok, n_tok), BF16),
        ),
        in_specs=[vmem] * 2 + [hbm] * 5,
        out_specs=(hbm, hbm, vmem, vmem),
        scratch_shapes=[
            pltpu.VMEM((n_tok, width), BF16),
            pltpu.VMEM((n_tok, width), BF16),
            pltpu.VMEM((half, 384), BF16),
            chunks(16),
            pltpu.VMEM((16, 16, 384), BF16),
            pltpu.VMEM((2, 64, 384), F32),
            pltpu.VMEM((2, 64, 384), BF16),
            pltpu.VMEM((2, 64, 384), BF16),
            chunks(16),
            chunks(8),
            chunks(4),
            chunks(4),
            chunks(4),
            chunks(4),
        ]
        + [pltpu.VMEM((16, half // 2), BF16)] * 4
        + [
            pltpu.SemaphoreType.DMA((7,)),
            pltpu.SemaphoreType.DMA((copies,)),
            pltpu.SemaphoreType.DMA((copies,)),
        ],
        compiler_params=pltpu.CompilerParams(
            collective_id=0, has_side_effects=True, vmem_limit_bytes=40 * 1024 * 1024
        ),
        cost_estimate=pl.CostEstimate(flops=400_000_000, bytes_accessed=6_000_000, transcendentals=16384),
        name="exchange",
    )(expert_ids, gate_fixed, tokens, out_cotangent, w_gate[0], w_up[0], w_down[0])
    steps = 2
    grad_spec = pl.BlockSpec((half // steps, 128), lambda i: (i, 0))
    tok_spec = pl.BlockSpec((n_tok, width // steps), lambda i: (0, i))
    layer_out, token_grad, gg, gu, gd = pl.pallas_call(
        output_kernel,
        grid=(steps,),
        out_shape=(jax.ShapeDtypeStruct((n_tok, width), BF16),) * 2
        + (jax.ShapeDtypeStruct((half, 128), F32),) * 3,
        in_specs=[
            pl.BlockSpec((256, half // steps), lambda i: (0, i)),
            pl.BlockSpec((256, 384), lambda i: (0, 0)),
            pl.BlockSpec((8, width // steps), lambda i: (0, i)),
            pl.BlockSpec((n_tok, n_tok), lambda i: (0, 0)),
        ],
        out_specs=(tok_spec, tok_spec, grad_spec, grad_spec, grad_spec),
        compiler_params=pltpu.CompilerParams(vmem_limit_bytes=32 * 1024 * 1024),
        cost_estimate=pl.CostEstimate(flops=400_000_000, bytes_accessed=6_000_000, transcendentals=0),
        name="outputs",
    )(x_all.reshape(256, half), act.reshape(256, 384), slots, sel)
    return (layer_out, token_grad, gg[None], gu[None], gd[None])


def solution(mesh):
    sizes = (mesh.shape["dp"], mesh.shape["expert"])
    return jax.shard_map(
        per_device_fused if sizes == (2, 16) else per_device,
        mesh=mesh,
        in_specs=(
            P(("dp", "expert"), None),
            P(("dp", "expert"), None),
            P(("dp", "expert"), None),
            P(("dp", "expert"), None),
            P("expert", "dp", None),
            P("expert", "dp", None),
            P("expert", "dp", None),
        ),
        out_specs=(
            P(("dp", "expert"), None),
            P(("dp", "expert"), None),
            P("expert", "dp", None),
            P("expert", "dp", None),
            P("expert", "dp", None),
        ),
        check_vma=False,
    )
```

```python
import jax
import jax.numpy as jnp
from jax import lax
from jax.sharding import PartitionSpec as P
from jax.experimental import pallas as pl
from jax.experimental.pallas import tpu as pltpu

SPLIT = 16
CAP = 4


SCALE = 2.0 ** (-16)
HIGH = lax.Precision.HIGHEST


def routing(ids, gates, window, capacity):
    wanted = jnp.arange(window, dtype=jnp.int32)
    hits = ids[:, :, None] == wanted[None, None, :]
    member = jnp.any(hits, axis=1)
    weight = jnp.sum(jnp.where(hits, gates[:, :, None], 0), axis=1).astype(jnp.float32) * SCALE
    rank = jnp.cumsum(member.astype(jnp.int32), axis=0) - 1
    slots = jnp.arange(capacity, dtype=jnp.int32)
    pick = jnp.logical_and(member[:, :, None], rank[:, :, None] == slots[None, None, :])
    select = jnp.where(pick, 1.0, 0.0).astype(jnp.float32)
    slot_gate = jnp.sum(select * weight[:, :, None], axis=0)
    return (select, slot_gate)


def expert_math(inputs, cotangents, gate_w, up_w, down_w):
    gate_pre = jnp.einsum("prf,pfh->rh", inputs, gate_w, preferred_element_type=jnp.float32)
    up_pre = jnp.einsum("prf,pfh->rh", inputs, up_w, preferred_element_type=jnp.float32)
    sig = jax.nn.sigmoid(gate_pre)
    act = gate_pre * sig
    hidden = (act * up_pre).astype(jnp.bfloat16)
    partial_out = jnp.einsum("rh,pfh->prf", hidden, down_w, preferred_element_type=jnp.float32)
    d_hidden = jnp.einsum("prf,pfh->rh", cotangents, down_w, preferred_element_type=jnp.float32)
    d_gate = (d_hidden * up_pre * sig * (1.0 + gate_pre * (1.0 - sig))).astype(jnp.bfloat16)
    d_up = (d_hidden * act).astype(jnp.bfloat16)
    partial_grad = jnp.einsum(
        "rh,pfh->prf", d_gate, gate_w, preferred_element_type=jnp.float32
    ) + jnp.einsum("rh,pfh->prf", d_up, up_w, preferred_element_type=jnp.float32)
    term = jnp.concatenate(
        [
            jnp.einsum("prf,rh->pfh", inputs, d_gate, preferred_element_type=jnp.float32),
            jnp.einsum("prf,rh->pfh", inputs, d_up, preferred_element_type=jnp.float32),
            jnp.einsum("prf,rh->pfh", cotangents, hidden, preferred_element_type=jnp.float32),
        ],
        axis=2,
    )
    return (partial_out, partial_grad, term.reshape(-1, term.shape[2]))


def per_device(tokens, out_cotangent, expert_ids, gate_fixed, w_gate, w_up, w_down):
    tok_rows, width = tokens.shape
    groups = lax.axis_size("expert")
    window = groups // SPLIT
    hid = w_gate.shape[2]
    parts = 1
    feat = width // parts
    select, slot_gate = routing(expert_ids, gate_fixed, window, CAP)
    select_b = select.astype(jnp.bfloat16)
    tok3 = tokens.reshape(tok_rows, parts, feat)
    cot3 = out_cotangent.reshape(tok_rows, parts, feat)
    slot_tokens = jnp.einsum(
        "tec,tsf->escf", select_b, tok3, preferred_element_type=jnp.float32
    ).astype(jnp.bfloat16)
    picked = jnp.einsum("tec,tsf->escf", select_b, cot3, preferred_element_type=jnp.float32)
    slot_cot = (picked * slot_gate[:, None, :, None]).astype(jnp.bfloat16)
    payload = jnp.stack([slot_tokens, slot_cot], axis=2)
    gate_full, up_full, down_full = (
        lax.all_gather(w_gate, "dp", axis=1, tiled=True),
        lax.all_gather(w_up, "dp", axis=1, tiled=True),
        lax.all_gather(w_down, "dp", axis=1, tiled=True),
    )
    outgoing = jnp.broadcast_to(payload, (window, SPLIT, 2, CAP, width)).reshape(
        groups, 2, CAP, width
    )
    arrived = lax.all_to_all(outgoing, "expert", split_axis=0, concat_axis=0, tiled=True)
    pieces = arrived[None]
    inputs = pieces[:, :, 0].reshape(parts, groups * CAP, feat)
    cotangents = pieces[:, :, 1].reshape(parts, groups * CAP, feat)
    partial_out, partial_grad, term = expert_math(inputs, cotangents, gate_full, up_full, down_full)
    summed = lax.psum_scatter(
        term.astype(jnp.bfloat16), "dp", scatter_dimension=0, tiled=True
    ).astype(jnp.float32)
    grad_gate = summed[:, :hid][None]
    grad_up = summed[:, hid : 2 * hid][None]
    grad_down = summed[:, 2 * hid :][None]
    results = jnp.stack(
        [
            partial_out.reshape(parts, groups, CAP, feat),
            partial_grad.reshape(parts, groups, CAP, feat),
        ],
        axis=2,
    )
    returned = lax.all_to_all(
        results[0].astype(jnp.bfloat16), "expert", split_axis=0, concat_axis=0, tiled=True
    ).astype(jnp.float32)
    combined = jnp.sum(
        returned.reshape(window, SPLIT, 2, CAP, width), axis=1, keepdims=True
    ).astype(jnp.bfloat16)
    weighted = select * slot_gate[None, :, :]
    layer_out = jnp.einsum(
        "tec,ehcf->thf", weighted, combined[:, :, 0].astype(jnp.float32), precision=HIGH
    )
    token_grad = jnp.einsum(
        "tec,ehcf->thf", select, combined[:, :, 1].astype(jnp.float32), precision=HIGH
    )
    return (
        layer_out.reshape(tok_rows, width).astype(jnp.bfloat16),
        token_grad.reshape(tok_rows, width).astype(jnp.bfloat16),
        grad_gate,
        grad_up,
        grad_down,
    )


MESH = pl.DeviceIdType.MESH
F32 = jnp.float32
BF16 = jnp.bfloat16


def row_ids(shape):
    return lax.broadcasted_iota(jnp.int32, shape, 0)


def fold(v):
    half = v.shape[1] // 2
    return jnp.concatenate([v[:, :half], v[:, half:]], axis=0)


def unfold(v):
    rows = v.shape[0] // 2
    return jnp.concatenate([v[:rows], v[rows:]], axis=1)


def exchange_kernel(
    ids_hbm, gates_hbm, tok_hbm, cot_hbm, wg_hbm, wu_hbm, wd_hbm,
    x_out, act_out, slot_out, sel_out,
    ids_v, gates_v, both_v, w_v, gath, rows_v, act_v, part, pex_s, pex_r, res, ra, sb, rb, sc, rc,
    across, load_sem, send_sem, recv_sem,
):
    y = lax.axis_index("dp")
    e = lax.axis_index("expert")
    z, x, c = e // 4, (e // 2) % 2, e % 2

    def dev(zz, xx, cc):
        return zz * 4 + xx * 2 + cc

    def pos(zz, xx, cc):
        return cc * 8 + xx * 4 + zz

    near = [z, z + 1 - 2 * (z % 2), (z + 2) % 4, 3 - z]
    peer_y = (1 - y, e)
    peer_c = (y, dev(z, x, 1 - c))
    peer_x = (y, dev(z, 1 - x, c))
    line = [[(yy, dev(zz, x, c)) for zz in near] for yy in (y, 1 - y)]

    started = []

    def remote(src, dst, target):
        n = len(started)
        copy = pltpu.make_async_remote_copy(
            src_ref=src, dst_ref=dst, send_sem=send_sem.at[n], recv_sem=recv_sem.at[n],
            device_id=target, device_id_type=MESH,
        )
        copy.start()
        started.append(copy)
        return copy

    n_tok = tok_hbm.shape[0]
    loads = [
        pltpu.make_async_copy(ids_hbm, ids_v, load_sem.at[0]),
        pltpu.make_async_copy(gates_hbm, gates_v, load_sem.at[1]),
        pltpu.make_async_copy(tok_hbm, both_v.at[:n_tok], load_sem.at[2]),
        pltpu.make_async_copy(cot_hbm, both_v.at[n_tok:], load_sem.at[3]),
        pltpu.make_async_copy(wg_hbm, w_v.at[:, 0:128], load_sem.at[4]),
        pltpu.make_async_copy(wu_hbm, w_v.at[:, 128:256], load_sem.at[5]),
        pltpu.make_async_copy(wd_hbm, w_v.at[:, 256:384], load_sem.at[6]),
    ]
    for load in loads:
        load.start()
    barrier = pltpu.get_barrier_semaphore()
    greeted = [peer_c, peer_x] + line[0][1:] + line[1]
    for target in greeted:
        pl.semaphore_signal(barrier, inc=1, device_id=target, device_id_type=MESH)

    square = (n_tok, n_tok)
    before = jnp.where(row_ids(square) < lax.broadcasted_iota(jnp.int32, square, 1), 1.0, 0.0).astype(BF16)
    loads[0].wait()
    loads[1].wait()
    hits = ids_v[...] == 0
    member = jnp.sum(jnp.where(hits, 1.0, 0.0), axis=0, keepdims=True)
    weight = jnp.sum(jnp.where(hits, gates_v[...].astype(F32), 0.0), axis=0, keepdims=True) * SCALE
    member8 = jnp.broadcast_to(member, (8, n_tok))
    rank = jnp.dot(member8.astype(BF16), before, preferred_element_type=F32)
    wanted = (row_ids((8, n_tok)) % CAP).astype(F32)
    sel = jnp.where(jnp.logical_and(rank == wanted, member8 > 0.5), 1.0, 0.0)
    sel_out[...] = sel
    gate8 = jnp.sum(sel * weight, axis=1, keepdims=True)
    nothing = jnp.zeros_like(sel)
    pick = jnp.concatenate(
        [jnp.concatenate([sel, nothing], axis=1), jnp.concatenate([nothing, sel], axis=1)], axis=0
    ).astype(BF16)
    loads[2].wait()
    loads[3].wait()
    slots = jnp.dot(pick, both_v[...], preferred_element_type=F32)
    half = slots.shape[1] // 2
    low = row_ids((8, half)) < 4
    piece_lo = jnp.where(low, slots[:8, :half], slots[8:, :half] * gate8)
    piece_hi = jnp.where(low, slots[:8, half:], slots[8:, half:] * gate8)
    here = pos(z, x, c)
    gath[here, y] = fold(jnp.where(y == 0, piece_lo, piece_hi)).astype(BF16)
    across[...] = fold(jnp.where(y == 0, piece_hi, piece_lo)).astype(BF16)
    pl.semaphore_wait(barrier, len(greeted))

    own = gath.at[here, y]
    over_z = [[None] * 4, [None] * 4]
    over_z[1][0] = remote(across, own, line[1][0])
    for k in (1, 2, 3):
        over_z[0][k] = remote(own, own, line[0][k])
        over_z[1][k] = remote(across, own, line[1][k])
    over_x, over_c = [], []
    for k in range(4):
        at = pos(near[k], x, c)
        for copy in (over_z[0][k], over_z[1][k]):
            if copy is not None:
                copy.wait_recv()
        over_x.append(remote(gath.at[at], gath.at[at], peer_x))
        over_c.append(remote(gath.at[at], gath.at[at], peer_c))
    for k in range(4):
        at = pos(near[k], 1 - x, c)
        over_x[k].wait_recv()
        over_c.append(remote(gath.at[at], gath.at[at], peer_c))

    for load in loads[4:]:
        load.wait()

    low3 = lax.broadcasted_iota(jnp.int32, (8, 8, 384), 1) < 4

    def project(h):
        for n in range(8):
            got = gath[h * 8 + n].astype(F32)
            rows_v[h * 8 + n] = jnp.concatenate([unfold(got[0]), unfold(got[1])], axis=0).astype(BF16)
        rows = rows_v[pl.ds(h * 8, 8)].reshape(128, half)
        p = jnp.dot(rows, w_v[...], preferred_element_type=F32).reshape(8, 2, 8, 384)
        p0, p1 = p[:, 0], p[:, 1]
        down1 = pltpu.roll(p1.reshape(64, 384), 4, 0).reshape(8, 8, 384)
        up0 = pltpu.roll(p0.reshape(64, 384), 60, 0).reshape(8, 8, 384)
        tok_part = jnp.where(low3, p0, down1)
        cot_part = jnp.where(low3, up0, p1)
        both = jnp.concatenate([tok_part[:, :, :256], cot_part[:, :, 256:]], axis=2).reshape(64, 384)
        part[h] = both
        pex_s[h] = both.astype(BF16)
        return remote(pex_s.at[h], pex_r.at[h], peer_y)

    def activate(h):
        total = part[h] + pex_r[h].astype(F32)
        gate_pre, up_pre, d_hidden = total[:, :128], total[:, 128:256], total[:, 256:]
        sig = jax.nn.sigmoid(gate_pre)
        act = gate_pre * sig
        hidden = (act * up_pre).astype(BF16)
        d_gate = (d_hidden * up_pre * sig * (1.0 + gate_pre * (1.0 - sig))).astype(BF16)
        d_up = (d_hidden * act).astype(BF16)
        d_both = jnp.concatenate([d_gate, d_up], axis=1)
        nt = (((1,), (1,)), ((), ()))
        out = lax.dot_general(hidden, w_v[:, 256:], nt, preferred_element_type=F32)
        grad = lax.dot_general(d_both, w_v[:, :256], nt, preferred_element_type=F32)
        res[pl.ds(h * 8, 8)] = jnp.concatenate(
            [out.reshape(8, 8, half), grad.reshape(8, 8, half)], axis=1
        ).astype(BF16)
        acts = jnp.concatenate([d_both, hidden], axis=1).astype(F32)
        up = pltpu.roll(acts, 60, 0).reshape(8, 8, 384)
        down = pltpu.roll(acts, 4, 0).reshape(8, 8, 384)
        acts = acts.reshape(8, 8, 384)
        for_tok = lax.broadcasted_iota(jnp.int32, (8, 8, 384), 2) < 256
        act_v[pl.ds(h * 8, 8)] = jnp.concatenate(
            [
                jnp.where(for_tok, jnp.where(low3, acts, 0.0), jnp.where(low3, 0.0, down)),
                jnp.where(for_tok, jnp.where(low3, up, 0.0), jnp.where(low3, 0.0, acts)),
            ],
            axis=1,
        ).astype(BF16)

    swap_own = project(c)
    for copy in over_c:
        copy.wait_recv()
    swap_other = project(1 - c)
    keep_x = pltpu.make_async_copy(rows_v, x_out, load_sem.at[7])
    keep_x.start()
    swap_other.wait_recv()
    activate(1 - c)
    to_core = []
    for xx in (1 - x, x):
        src = res.at[pl.ds((1 - c) * 8 + xx * 4, 4)]
        to_core.append(remote(src, ra.at[pl.ds(xx * 4, 4)], peer_c))
    swap_own.wait_recv()
    activate(c)
    keep_act = pltpu.make_async_copy(act_v, act_out, load_sem.at[8])
    keep_act.start()
    to_core[0].wait_recv()
    to_x = [None] * 4
    for k in (3, 2, 1, 0):
        zz = near[k]
        sb[k] = (res[pos(zz, 1 - x, c)].astype(F32) + ra[(1 - x) * 4 + zz].astype(F32)).astype(BF16)
        to_x[k] = remote(sb.at[k], rb.at[k], peer_x)
    to_core[1].wait_recv()

    def summed(k):
        zz = near[k]
        mid = res[pos(zz, x, c)].astype(F32) + ra[x * 4 + zz].astype(F32)
        to_x[k].wait_recv()
        mid = mid + rb[k].astype(F32)
        out8, grad8 = mid[:8], mid[8:]
        for_0 = jnp.where(low, out8, pltpu.roll(grad8, 4, 0))
        for_1 = jnp.where(low, pltpu.roll(out8, 4, 0), grad8)
        return jnp.where(y == 0, for_0, for_1), jnp.where(y == 0, for_1, for_0)

    to_z = []
    for k in (3, 2, 1, 0):
        same, other = summed(k)
        sc[1, k] = fold(other).astype(BF16)
        to_z.append((1, k, remote(sc.at[1, k], rc.at[1, k], line[1][k])))
        if k:
            sc[0, k] = fold(same).astype(BF16)
            to_z.append((0, k, remote(sc.at[0, k], rc.at[0, k], line[0][k])))
    total = [same, jnp.zeros_like(same)]
    for s_y, k, copy in to_z:
        copy.wait_recv()
        total[s_y] = total[s_y] + unfold(rc[s_y, k].astype(F32))
    mine8, got8 = (t.astype(BF16).astype(F32) for t in total)
    scale = jnp.where(row_ids((8, 1)) < 4, gate8, 1.0)
    slot_out[:, :half] = jnp.where(y == 0, mine8, got8) * scale
    slot_out[:, half:] = jnp.where(y == 0, got8, mine8) * scale
    keep_x.wait()
    keep_act.wait()
    for copy in started:
        copy.wait_send()


def output_kernel(x_ref, act_ref, slot_ref, sel_ref, out_ref, tg_ref, gg_ref, gu_ref, gd_ref):
    sel = sel_ref[...]
    low = row_ids(sel.shape) < 4
    slots = slot_ref[...].astype(BF16)
    tn = (((0,), (0,)), ((), ()))
    for ref, keep in ((out_ref, low), (tg_ref, jnp.logical_not(low))):
        picks = jnp.where(keep, sel, 0.0).astype(BF16)
        ref[...] = lax.dot_general(picks, slots, tn, preferred_element_type=F32).astype(BF16)
    grads = lax.dot_general(x_ref[...], act_ref[...], tn, preferred_element_type=F32)
    for n, ref in enumerate((gg_ref, gu_ref, gd_ref)):
        ref[...] = grads[:, n * 128 : (n + 1) * 128]


def per_device_fused(tokens, out_cotangent, expert_ids, gate_fixed, w_gate, w_up, w_down):
    n_tok, width = tokens.shape
    half = width // 2
    hbm = pl.BlockSpec(memory_space=pltpu.HBM)
    vmem = pl.BlockSpec(memory_space=pltpu.VMEM)
    copies = 35
    chunks = lambda n: pltpu.VMEM((n, 16, half), BF16)
    pieces = lambda m, n: pltpu.VMEM((m, n, 16, half // 2), BF16)
    x_all, act, slots, sel = pl.pallas_call(
        exchange_kernel,
        out_shape=(
            jax.ShapeDtypeStruct((16, 16, half), BF16),
            jax.ShapeDtypeStruct((16, 16, 384), BF16),
            jax.ShapeDtypeStruct((8, width), F32),
            jax.ShapeDtypeStruct((8, n_tok), F32),
        ),
        in_specs=[hbm] * 7,
        out_specs=(hbm, hbm, vmem, vmem),
        scratch_shapes=[
            pltpu.VMEM(expert_ids.shape[::-1], jnp.int32),
            pltpu.VMEM(gate_fixed.shape[::-1], jnp.int32),
            pltpu.VMEM((2 * n_tok, width), BF16),
            pltpu.VMEM((half, 384), BF16),
            pieces(16, 2),
            chunks(16),
            pltpu.VMEM((16, 16, 384), BF16),
            pltpu.VMEM((2, 64, 384), F32),
            pltpu.VMEM((2, 64, 384), BF16),
            pltpu.VMEM((2, 64, 384), BF16),
            chunks(16),
            chunks(8),
            chunks(4),
            chunks(4),
            pieces(2, 4),
            pieces(2, 4),
            pltpu.VMEM((16, half // 2), BF16),
            pltpu.SemaphoreType.DMA((9,)),
            pltpu.SemaphoreType.DMA((copies,)),
            pltpu.SemaphoreType.DMA((copies,)),
        ],
        compiler_params=pltpu.CompilerParams(
            collective_id=0, has_side_effects=True, vmem_limit_bytes=60 * 1024 * 1024
        ),
        cost_estimate=pl.CostEstimate(flops=400_000_000, bytes_accessed=6_000_000, transcendentals=16384),
        name="exchange",
    )(expert_ids.T, gate_fixed.T, tokens, out_cotangent, w_gate[0], w_up[0], w_down[0])
    steps = 2
    grad_spec = pl.BlockSpec((half // steps, 128), lambda i: (i, 0))
    tok_spec = pl.BlockSpec((n_tok, width // steps), lambda i: (0, i))
    layer_out, token_grad, gg, gu, gd = pl.pallas_call(
        output_kernel,
        grid=(steps,),
        out_shape=(jax.ShapeDtypeStruct((n_tok, width), BF16),) * 2
        + (jax.ShapeDtypeStruct((half, 128), F32),) * 3,
        in_specs=[
            pl.BlockSpec((256, half // steps), lambda i: (0, i)),
            pl.BlockSpec((256, 384), lambda i: (0, 0)),
            pl.BlockSpec((8, width // steps), lambda i: (0, i)),
            pl.BlockSpec((8, n_tok), lambda i: (0, 0)),
        ],
        out_specs=(tok_spec, tok_spec, grad_spec, grad_spec, grad_spec),
        compiler_params=pltpu.CompilerParams(vmem_limit_bytes=60 * 1024 * 1024),
        cost_estimate=pl.CostEstimate(flops=400_000_000, bytes_accessed=6_000_000, transcendentals=0),
        name="outputs",
    )(x_all.reshape(256, half), act.reshape(256, 384), slots, sel)
    return (layer_out, token_grad, gg[None], gu[None], gd[None])


def solution(mesh):
    sizes = (mesh.shape["dp"], mesh.shape["expert"])
    return jax.shard_map(
        per_device_fused if sizes == (2, 16) else per_device,
        mesh=mesh,
        in_specs=(
            P(("dp", "expert"), None),
            P(("dp", "expert"), None),
            P(("dp", "expert"), None),
            P(("dp", "expert"), None),
            P("expert", "dp", None),
            P("expert", "dp", None),
            P("expert", "dp", None),
        ),
        out_specs=(
            P(("dp", "expert"), None),
            P(("dp", "expert"), None),
            P("expert", "dp", None),
            P("expert", "dp", None),
            P("expert", "dp", None),
        ),
        check_vma=False,
    )
```

```python
import jax
import jax.numpy as jnp
from jax import lax
from jax.sharding import PartitionSpec as P
from jax.experimental import pallas as pl
from jax.experimental.pallas import tpu as pltpu

SPLIT = 16
CAP = 4


SCALE = 2.0 ** (-16)
HIGH = lax.Precision.HIGHEST


def routing(ids, gates, window, capacity):
    wanted = jnp.arange(window, dtype=jnp.int32)
    hits = ids[:, :, None] == wanted[None, None, :]
    member = jnp.any(hits, axis=1)
    weight = jnp.sum(jnp.where(hits, gates[:, :, None], 0), axis=1).astype(jnp.float32) * SCALE
    rank = jnp.cumsum(member.astype(jnp.int32), axis=0) - 1
    slots = jnp.arange(capacity, dtype=jnp.int32)
    pick = jnp.logical_and(member[:, :, None], rank[:, :, None] == slots[None, None, :])
    select = jnp.where(pick, 1.0, 0.0).astype(jnp.float32)
    slot_gate = jnp.sum(select * weight[:, :, None], axis=0)
    return (select, slot_gate)


def expert_math(inputs, cotangents, gate_w, up_w, down_w):
    gate_pre = jnp.einsum("prf,pfh->rh", inputs, gate_w, preferred_element_type=jnp.float32)
    up_pre = jnp.einsum("prf,pfh->rh", inputs, up_w, preferred_element_type=jnp.float32)
    sig = jax.nn.sigmoid(gate_pre)
    act = gate_pre * sig
    hidden = (act * up_pre).astype(jnp.bfloat16)
    partial_out = jnp.einsum("rh,pfh->prf", hidden, down_w, preferred_element_type=jnp.float32)
    d_hidden = jnp.einsum("prf,pfh->rh", cotangents, down_w, preferred_element_type=jnp.float32)
    d_gate = (d_hidden * up_pre * sig * (1.0 + gate_pre * (1.0 - sig))).astype(jnp.bfloat16)
    d_up = (d_hidden * act).astype(jnp.bfloat16)
    partial_grad = jnp.einsum(
        "rh,pfh->prf", d_gate, gate_w, preferred_element_type=jnp.float32
    ) + jnp.einsum("rh,pfh->prf", d_up, up_w, preferred_element_type=jnp.float32)
    term = jnp.concatenate(
        [
            jnp.einsum("prf,rh->pfh", inputs, d_gate, preferred_element_type=jnp.float32),
            jnp.einsum("prf,rh->pfh", inputs, d_up, preferred_element_type=jnp.float32),
            jnp.einsum("prf,rh->pfh", cotangents, hidden, preferred_element_type=jnp.float32),
        ],
        axis=2,
    )
    return (partial_out, partial_grad, term.reshape(-1, term.shape[2]))


def per_device(tokens, out_cotangent, expert_ids, gate_fixed, w_gate, w_up, w_down):
    tok_rows, width = tokens.shape
    groups = lax.axis_size("expert")
    window = groups // SPLIT
    hid = w_gate.shape[2]
    parts = 1
    feat = width // parts
    select, slot_gate = routing(expert_ids, gate_fixed, window, CAP)
    select_b = select.astype(jnp.bfloat16)
    tok3 = tokens.reshape(tok_rows, parts, feat)
    cot3 = out_cotangent.reshape(tok_rows, parts, feat)
    slot_tokens = jnp.einsum(
        "tec,tsf->escf", select_b, tok3, preferred_element_type=jnp.float32
    ).astype(jnp.bfloat16)
    picked = jnp.einsum("tec,tsf->escf", select_b, cot3, preferred_element_type=jnp.float32)
    slot_cot = (picked * slot_gate[:, None, :, None]).astype(jnp.bfloat16)
    payload = jnp.stack([slot_tokens, slot_cot], axis=2)
    gate_full, up_full, down_full = (
        lax.all_gather(w_gate, "dp", axis=1, tiled=True),
        lax.all_gather(w_up, "dp", axis=1, tiled=True),
        lax.all_gather(w_down, "dp", axis=1, tiled=True),
    )
    outgoing = jnp.broadcast_to(payload, (window, SPLIT, 2, CAP, width)).reshape(
        groups, 2, CAP, width
    )
    arrived = lax.all_to_all(outgoing, "expert", split_axis=0, concat_axis=0, tiled=True)
    pieces = arrived[None]
    inputs = pieces[:, :, 0].reshape(parts, groups * CAP, feat)
    cotangents = pieces[:, :, 1].reshape(parts, groups * CAP, feat)
    partial_out, partial_grad, term = expert_math(inputs, cotangents, gate_full, up_full, down_full)
    summed = lax.psum_scatter(
        term.astype(jnp.bfloat16), "dp", scatter_dimension=0, tiled=True
    ).astype(jnp.float32)
    grad_gate = summed[:, :hid][None]
    grad_up = summed[:, hid : 2 * hid][None]
    grad_down = summed[:, 2 * hid :][None]
    results = jnp.stack(
        [
            partial_out.reshape(parts, groups, CAP, feat),
            partial_grad.reshape(parts, groups, CAP, feat),
        ],
        axis=2,
    )
    returned = lax.all_to_all(
        results[0].astype(jnp.bfloat16), "expert", split_axis=0, concat_axis=0, tiled=True
    ).astype(jnp.float32)
    combined = jnp.sum(
        returned.reshape(window, SPLIT, 2, CAP, width), axis=1, keepdims=True
    ).astype(jnp.bfloat16)
    weighted = select * slot_gate[None, :, :]
    layer_out = jnp.einsum(
        "tec,ehcf->thf", weighted, combined[:, :, 0].astype(jnp.float32), precision=HIGH
    )
    token_grad = jnp.einsum(
        "tec,ehcf->thf", select, combined[:, :, 1].astype(jnp.float32), precision=HIGH
    )
    return (
        layer_out.reshape(tok_rows, width).astype(jnp.bfloat16),
        token_grad.reshape(tok_rows, width).astype(jnp.bfloat16),
        grad_gate,
        grad_up,
        grad_down,
    )


MESH = pl.DeviceIdType.MESH
F32 = jnp.float32
BF16 = jnp.bfloat16


def row_ids(shape):
    return lax.broadcasted_iota(jnp.int32, shape, 0)


def fold(v):
    half = v.shape[1] // 2
    return jnp.concatenate([v[:, :half], v[:, half:]], axis=0)


def unfold(v):
    rows = v.shape[0] // 2
    return jnp.concatenate([v[:rows], v[rows:]], axis=1)


def exchange_kernel(
    ids_hbm, gates_hbm, tok_hbm, cot_hbm, wg_hbm, wu_hbm, wd_hbm,
    gg_out, gu_out, gd_out, slot_out, sel_out,
    ids_v, gates_v, both_v, w_v, gath, rows_v, act_v, part, pex_s, pex_r, res, ra, sb, rb, sc, rc,
    across, grad_v, load_sem, send_sem, recv_sem,
):
    y = lax.axis_index("dp")
    e = lax.axis_index("expert")
    z, x, c = e // 4, (e // 2) % 2, e % 2

    def dev(zz, xx, cc):
        return zz * 4 + xx * 2 + cc

    def pos(zz, xx, cc):
        return (zz // 2) * 8 + cc * 4 + xx * 2 + zz % 2

    near = [z, z + 1 - 2 * (z % 2), (z + 2) % 4, 3 - z]
    peer_y = (1 - y, e)
    peer_c = (y, dev(z, x, 1 - c))
    peer_x = (y, dev(z, 1 - x, c))
    line = [[(yy, dev(zz, x, c)) for zz in near] for yy in (y, 1 - y)]

    started = []

    def remote(src, dst, target):
        n = len(started)
        copy = pltpu.make_async_remote_copy(
            src_ref=src, dst_ref=dst, send_sem=send_sem.at[n], recv_sem=recv_sem.at[n],
            device_id=target, device_id_type=MESH,
        )
        copy.start()
        started.append(copy)
        return copy

    n_tok = tok_hbm.shape[0]
    loads = [
        pltpu.make_async_copy(ids_hbm, ids_v, load_sem.at[0]),
        pltpu.make_async_copy(gates_hbm, gates_v, load_sem.at[1]),
        pltpu.make_async_copy(tok_hbm, both_v.at[:n_tok], load_sem.at[2]),
        pltpu.make_async_copy(cot_hbm, both_v.at[n_tok:], load_sem.at[3]),
        pltpu.make_async_copy(wg_hbm, w_v.at[:, 0:128], load_sem.at[4]),
        pltpu.make_async_copy(wu_hbm, w_v.at[:, 128:256], load_sem.at[5]),
        pltpu.make_async_copy(wd_hbm, w_v.at[:, 256:384], load_sem.at[6]),
    ]
    for load in loads:
        load.start()
    barrier = pltpu.get_barrier_semaphore()
    greeted = [peer_c, peer_x] + line[0][1:] + line[1]
    for target in greeted:
        pl.semaphore_signal(barrier, inc=1, device_id=target, device_id_type=MESH)

    square = (n_tok, n_tok)
    before = jnp.where(row_ids(square) < lax.broadcasted_iota(jnp.int32, square, 1), 1.0, 0.0).astype(BF16)
    loads[0].wait()
    loads[1].wait()
    hits = ids_v[...] == 0
    member = jnp.sum(jnp.where(hits, 1.0, 0.0), axis=0, keepdims=True)
    weight = jnp.sum(jnp.where(hits, gates_v[...].astype(F32), 0.0), axis=0, keepdims=True) * SCALE
    member8 = jnp.broadcast_to(member, (8, n_tok))
    rank = jnp.dot(member8.astype(BF16), before, preferred_element_type=F32)
    wanted = (row_ids((8, n_tok)) % CAP).astype(F32)
    sel = jnp.where(jnp.logical_and(rank == wanted, member8 > 0.5), 1.0, 0.0)
    sel_out[...] = sel
    gate8 = jnp.sum(sel * weight, axis=1, keepdims=True)
    nothing = jnp.zeros_like(sel)
    pick = jnp.concatenate(
        [jnp.concatenate([sel, nothing], axis=1), jnp.concatenate([nothing, sel], axis=1)], axis=0
    ).astype(BF16)
    loads[2].wait()
    loads[3].wait()
    slots = jnp.dot(pick, both_v[...], preferred_element_type=F32)
    half = slots.shape[1] // 2
    low = row_ids((8, half)) < 4
    piece_lo = jnp.where(low, slots[:8, :half], slots[8:, :half] * gate8)
    piece_hi = jnp.where(low, slots[:8, half:], slots[8:, half:] * gate8)
    here = pos(z, x, c)
    gath[here, y] = fold(jnp.where(y == 0, piece_lo, piece_hi)).astype(BF16)
    across[...] = fold(jnp.where(y == 0, piece_hi, piece_lo)).astype(BF16)
    pl.semaphore_wait(barrier, len(greeted))

    own = gath.at[here, y]
    over_z = [[None] * 4, [None] * 4]
    for k in (1, 0, 2, 3):
        if k:
            over_z[0][k] = remote(own, own, line[0][k])
        over_z[1][k] = remote(across, own, line[1][k])
    over_x, over_c = [], [[], []]

    def forward(k):
        at = pos(near[k], x, c)
        for copy in (over_z[0][k], over_z[1][k]):
            if copy is not None:
                copy.wait_recv()
        over_x.append(remote(gath.at[at], gath.at[at], peer_x))
        over_c[k // 2].append(remote(gath.at[at], gath.at[at], peer_c))

    def forward_x(k):
        at = pos(near[k], 1 - x, c)
        over_x[k].wait_recv()
        over_c[k // 2].append(remote(gath.at[at], gath.at[at], peer_c))

    low3 = lax.broadcasted_iota(jnp.int32, (8, 8, 384), 1) < 4

    def project(h):
        for n in range(8):
            got = gath[h * 8 + n].astype(F32)
            rows_v[h * 8 + n] = jnp.concatenate([unfold(got[0]), unfold(got[1])], axis=0).astype(BF16)
        rows = rows_v[pl.ds(h * 8, 8)].reshape(128, half)
        p = jnp.dot(rows, w_v[...], preferred_element_type=F32).reshape(8, 2, 8, 384)
        p0, p1 = p[:, 0], p[:, 1]
        down1 = pltpu.roll(p1.reshape(64, 384), 4, 0).reshape(8, 8, 384)
        up0 = pltpu.roll(p0.reshape(64, 384), 60, 0).reshape(8, 8, 384)
        tok_part = jnp.where(low3, p0, down1)
        cot_part = jnp.where(low3, up0, p1)
        both = jnp.concatenate([tok_part[:, :, :256], cot_part[:, :, 256:]], axis=2).reshape(64, 384)
        part[h] = both
        pex_s[h] = both.astype(BF16)
        return remote(pex_s.at[h], pex_r.at[h], peer_y)

    def activate(h):
        total = part[h] + pex_r[h].astype(F32)
        gate_pre, up_pre, d_hidden = total[:, :128], total[:, 128:256], total[:, 256:]
        sig = jax.nn.sigmoid(gate_pre)
        act = gate_pre * sig
        hidden = (act * up_pre).astype(BF16)
        d_gate = (d_hidden * up_pre * sig * (1.0 + gate_pre * (1.0 - sig))).astype(BF16)
        d_up = (d_hidden * act).astype(BF16)
        d_both = jnp.concatenate([d_gate, d_up], axis=1)
        nt = (((1,), (1,)), ((), ()))
        out = lax.dot_general(hidden, w_v[:, 256:], nt, preferred_element_type=F32)
        grad = lax.dot_general(d_both, w_v[:, :256], nt, preferred_element_type=F32)
        res[pl.ds(h * 8, 8)] = jnp.concatenate(
            [out.reshape(8, 8, half), grad.reshape(8, 8, half)], axis=1
        ).astype(BF16)
        acts = jnp.concatenate([d_both, hidden], axis=1).astype(F32)
        up = pltpu.roll(acts, 60, 0).reshape(8, 8, 384)
        down = pltpu.roll(acts, 4, 0).reshape(8, 8, 384)
        acts = acts.reshape(8, 8, 384)
        for_tok = lax.broadcasted_iota(jnp.int32, (8, 8, 384), 2) < 256
        act_v[pl.ds(h * 8, 8)] = jnp.concatenate(
            [
                jnp.where(for_tok, jnp.where(low3, acts, 0.0), jnp.where(low3, 0.0, down)),
                jnp.where(for_tok, jnp.where(low3, up, 0.0), jnp.where(low3, 0.0, acts)),
            ],
            axis=1,
        ).astype(BF16)

    def core_chunks(part_of):
        for copy in over_c[part_of]:
            copy.wait_recv()

    def to_core(pair):
        src = res.at[pl.ds(pair * 8 + (1 - c) * 4, 4)]
        return remote(src, ra.at[pl.ds(pair * 4, 4)], peer_c)

    def core_sum(k, xx):
        zz = near[k]
        return res[pos(zz, xx, c)].astype(F32) + ra[(zz // 2) * 4 + xx * 2 + zz % 2].astype(F32)

    to_x = [None] * 4

    def send_x(k):
        sb[k] = core_sum(k, 1 - x).astype(BF16)
        to_x[k] = remote(sb.at[k], rb.at[k], peer_x)

    grad_copies = []

    def gradients(n):
        cols = half // 2
        rows = rows_v[:, :, n * cols : (n + 1) * cols].reshape(256, cols)
        tn = (((0,), (0,)), ((), ()))
        terms = lax.dot_general(rows, act_v[...].reshape(256, 384), tn, preferred_element_type=F32)
        for i, out in enumerate((gg_out, gu_out, gd_out)):
            at = pl.ds(n * cols, cols)
            grad_v[i, at] = terms[:, i * 128 : (i + 1) * 128]
            copy = pltpu.make_async_copy(grad_v.at[i, at], out.at[at], load_sem.at[7 + 3 * n + i])
            copy.start()
            grad_copies.append(copy)

    def summed(k):
        mid = core_sum(k, x)
        to_x[k].wait_recv()
        mid = mid + rb[k].astype(F32)
        out8, grad8 = mid[:8], mid[8:]
        for_0 = jnp.where(low, out8, pltpu.roll(grad8, 4, 0))
        for_1 = jnp.where(low, pltpu.roll(out8, 4, 0), grad8)
        return jnp.where(y == 0, for_0, for_1), jnp.where(y == 0, for_1, for_0)

    to_z = []

    def send_z(k):
        same, other = summed(k)
        sc[1, k] = fold(other).astype(BF16)
        to_z.append((1, k, remote(sc.at[1, k], rc.at[1, k], line[1][k])))
        if k:
            sc[0, k] = fold(same).astype(BF16)
            to_z.append((0, k, remote(sc.at[0, k], rc.at[0, k], line[0][k])))
        return same

    pair = z // 2
    forward(0)
    forward(1)
    forward_x(0)
    forward_x(1)
    forward(2)
    for load in loads[4:]:
        load.wait()
    core_chunks(0)
    swap_near = project(pair)
    forward(3)
    forward_x(2)
    forward_x(3)
    core_chunks(1)
    swap_far = project(1 - pair)
    swap_near.wait_recv()
    activate(pair)
    core_near = to_core(pair)
    core_near.wait_recv()
    send_x(1)
    send_x(0)
    swap_far.wait_recv()
    activate(1 - pair)
    core_far = to_core(1 - pair)
    gradients(0)
    core_far.wait_recv()
    send_x(3)
    send_x(2)
    send_z(1)
    same = send_z(0)
    gradients(1)
    send_z(3)
    send_z(2)
    total = [same, jnp.zeros_like(same)]
    for s_y, k, copy in to_z:
        copy.wait_recv()
        total[s_y] = total[s_y] + unfold(rc[s_y, k].astype(F32))
    mine8, got8 = (t.astype(BF16).astype(F32) for t in total)
    scale = jnp.where(row_ids((8, 1)) < 4, gate8, 1.0)
    slot_out[:, :half] = jnp.where(y == 0, mine8, got8) * scale
    slot_out[:, half:] = jnp.where(y == 0, got8, mine8) * scale
    for copy in grad_copies:
        copy.wait()
    for copy in started:
        copy.wait_send()


def output_kernel(slot_ref, sel_ref, gg_in, gu_in, gd_in, out_ref, tg_ref, gg_ref, gu_ref, gd_ref, rows, sems):
    copies = []

    def move(src, dst):
        copy = pltpu.make_async_copy(src, dst, sems.at[len(copies)])
        copy.start()
        copies.append(copy)

    cut = gg_in.shape[0] // 2
    for n in range(2):
        for src, dst in ((gg_in, gg_ref), (gu_in, gu_ref), (gd_in, gd_ref)):
            move(src.at[pl.ds(n * cut, cut)], dst.at[pl.ds(n * cut, cut)])
    sel = sel_ref[...]
    low = row_ids(sel.shape) < 4
    slots = slot_ref[...].astype(BF16)
    tn = (((0,), (0,)), ((), ()))
    for n, (ref, keep) in enumerate(((out_ref, low), (tg_ref, jnp.logical_not(low)))):
        picks = jnp.where(keep, sel, 0.0).astype(BF16)
        rows[n] = lax.dot_general(picks, slots, tn, preferred_element_type=F32).astype(BF16)
        move(rows.at[n], ref)
    for copy in copies:
        copy.wait()


def per_device_fused(tokens, out_cotangent, expert_ids, gate_fixed, w_gate, w_up, w_down):
    n_tok, width = tokens.shape
    half = width // 2
    hbm = pl.BlockSpec(memory_space=pltpu.HBM)
    vmem = pl.BlockSpec(memory_space=pltpu.VMEM)
    copies = 35
    chunks = lambda n: pltpu.VMEM((n, 16, half), BF16)
    pieces = lambda m, n: pltpu.VMEM((m, n, 16, half // 2), BF16)
    gg, gu, gd, slots, sel = pl.pallas_call(
        exchange_kernel,
        out_shape=(
            *[jax.ShapeDtypeStruct((half, 128), F32)] * 3,
            jax.ShapeDtypeStruct((8, width), F32),
            jax.ShapeDtypeStruct((8, n_tok), F32),
        ),
        in_specs=[hbm] * 7,
        out_specs=(hbm, hbm, hbm, vmem, vmem),
        scratch_shapes=[
            pltpu.VMEM(expert_ids.shape[::-1], jnp.int32),
            pltpu.VMEM(gate_fixed.shape[::-1], jnp.int32),
            pltpu.VMEM((2 * n_tok, width), BF16),
            pltpu.VMEM((half, 384), BF16),
            pieces(16, 2),
            chunks(16),
            pltpu.VMEM((16, 16, 384), BF16),
            pltpu.VMEM((2, 64, 384), F32),
            pltpu.VMEM((2, 64, 384), BF16),
            pltpu.VMEM((2, 64, 384), BF16),
            chunks(16),
            chunks(8),
            chunks(4),
            chunks(4),
            pieces(2, 4),
            pieces(2, 4),
            pltpu.VMEM((16, half // 2), BF16),
            pltpu.VMEM((3, half, 128), F32),
            pltpu.SemaphoreType.DMA((13,)),
            pltpu.SemaphoreType.DMA((copies,)),
            pltpu.SemaphoreType.DMA((copies,)),
        ],
        compiler_params=pltpu.CompilerParams(
            collective_id=0, has_side_effects=True, vmem_limit_bytes=60 * 1024 * 1024
        ),
        cost_estimate=pl.CostEstimate(flops=400_000_000, bytes_accessed=6_000_000, transcendentals=16384),
        name="exchange",
    )(expert_ids.T, gate_fixed.T, tokens, out_cotangent, w_gate[0], w_up[0], w_down[0])
    layer_out, token_grad, gg, gu, gd = pl.pallas_call(
        output_kernel,
        out_shape=(jax.ShapeDtypeStruct((n_tok, width), BF16),) * 2
        + (jax.ShapeDtypeStruct((half, 128), F32),) * 3,
        in_specs=[vmem, vmem, hbm, hbm, hbm],
        out_specs=(hbm,) * 5,
        scratch_shapes=[pltpu.VMEM((2, n_tok, width), BF16), pltpu.SemaphoreType.DMA((8,))],
        compiler_params=pltpu.CompilerParams(vmem_limit_bytes=60 * 1024 * 1024),
        cost_estimate=pl.CostEstimate(flops=15_000_000, bytes_accessed=8_000_000, transcendentals=0),
        name="outputs",
    )(slots, sel, gg, gu, gd)
    return (layer_out, token_grad, gg[None], gu[None], gd[None])


def solution(mesh):
    sizes = (mesh.shape["dp"], mesh.shape["expert"])
    return jax.shard_map(
        per_device_fused if sizes == (2, 16) else per_device,
        mesh=mesh,
        in_specs=(
            P(("dp", "expert"), None),
            P(("dp", "expert"), None),
            P(("dp", "expert"), None),
            P(("dp", "expert"), None),
            P("expert", "dp", None),
            P("expert", "dp", None),
            P("expert", "dp", None),
        ),
        out_specs=(
            P(("dp", "expert"), None),
            P(("dp", "expert"), None),
            P("expert", "dp", None),
            P("expert", "dp", None),
            P("expert", "dp", None),
        ),
        check_vma=False,
    )
```

```python
import jax
import jax.numpy as jnp
from jax import lax
from jax.sharding import PartitionSpec as P
from jax.experimental import pallas as pl
from jax.experimental.pallas import tpu as pltpu

SPLIT = 16
CAP = 4


SCALE = 2.0 ** (-16)
HIGH = lax.Precision.HIGHEST


def routing(ids, gates, window, capacity):
    wanted = jnp.arange(window, dtype=jnp.int32)
    hits = ids[:, :, None] == wanted[None, None, :]
    member = jnp.any(hits, axis=1)
    weight = jnp.sum(jnp.where(hits, gates[:, :, None], 0), axis=1).astype(jnp.float32) * SCALE
    rank = jnp.cumsum(member.astype(jnp.int32), axis=0) - 1
    slots = jnp.arange(capacity, dtype=jnp.int32)
    pick = jnp.logical_and(member[:, :, None], rank[:, :, None] == slots[None, None, :])
    select = jnp.where(pick, 1.0, 0.0).astype(jnp.float32)
    slot_gate = jnp.sum(select * weight[:, :, None], axis=0)
    return (select, slot_gate)


def expert_math(inputs, cotangents, gate_w, up_w, down_w):
    gate_pre = jnp.einsum("prf,pfh->rh", inputs, gate_w, preferred_element_type=jnp.float32)
    up_pre = jnp.einsum("prf,pfh->rh", inputs, up_w, preferred_element_type=jnp.float32)
    sig = jax.nn.sigmoid(gate_pre)
    act = gate_pre * sig
    hidden = (act * up_pre).astype(jnp.bfloat16)
    partial_out = jnp.einsum("rh,pfh->prf", hidden, down_w, preferred_element_type=jnp.float32)
    d_hidden = jnp.einsum("prf,pfh->rh", cotangents, down_w, preferred_element_type=jnp.float32)
    d_gate = (d_hidden * up_pre * sig * (1.0 + gate_pre * (1.0 - sig))).astype(jnp.bfloat16)
    d_up = (d_hidden * act).astype(jnp.bfloat16)
    partial_grad = jnp.einsum(
        "rh,pfh->prf", d_gate, gate_w, preferred_element_type=jnp.float32
    ) + jnp.einsum("rh,pfh->prf", d_up, up_w, preferred_element_type=jnp.float32)
    term = jnp.concatenate(
        [
            jnp.einsum("prf,rh->pfh", inputs, d_gate, preferred_element_type=jnp.float32),
            jnp.einsum("prf,rh->pfh", inputs, d_up, preferred_element_type=jnp.float32),
            jnp.einsum("prf,rh->pfh", cotangents, hidden, preferred_element_type=jnp.float32),
        ],
        axis=2,
    )
    return (partial_out, partial_grad, term.reshape(-1, term.shape[2]))


def per_device(tokens, out_cotangent, expert_ids, gate_fixed, w_gate, w_up, w_down):
    tok_rows, width = tokens.shape
    groups = lax.axis_size("expert")
    window = groups // SPLIT
    hid = w_gate.shape[2]
    parts = 1
    feat = width // parts
    select, slot_gate = routing(expert_ids, gate_fixed, window, CAP)
    select_b = select.astype(jnp.bfloat16)
    tok3 = tokens.reshape(tok_rows, parts, feat)
    cot3 = out_cotangent.reshape(tok_rows, parts, feat)
    slot_tokens = jnp.einsum(
        "tec,tsf->escf", select_b, tok3, preferred_element_type=jnp.float32
    ).astype(jnp.bfloat16)
    picked = jnp.einsum("tec,tsf->escf", select_b, cot3, preferred_element_type=jnp.float32)
    slot_cot = (picked * slot_gate[:, None, :, None]).astype(jnp.bfloat16)
    payload = jnp.stack([slot_tokens, slot_cot], axis=2)
    gate_full, up_full, down_full = (
        lax.all_gather(w_gate, "dp", axis=1, tiled=True),
        lax.all_gather(w_up, "dp", axis=1, tiled=True),
        lax.all_gather(w_down, "dp", axis=1, tiled=True),
    )
    outgoing = jnp.broadcast_to(payload, (window, SPLIT, 2, CAP, width)).reshape(
        groups, 2, CAP, width
    )
    arrived = lax.all_to_all(outgoing, "expert", split_axis=0, concat_axis=0, tiled=True)
    pieces = arrived[None]
    inputs = pieces[:, :, 0].reshape(parts, groups * CAP, feat)
    cotangents = pieces[:, :, 1].reshape(parts, groups * CAP, feat)
    partial_out, partial_grad, term = expert_math(inputs, cotangents, gate_full, up_full, down_full)
    summed = lax.psum_scatter(
        term.astype(jnp.bfloat16), "dp", scatter_dimension=0, tiled=True
    ).astype(jnp.float32)
    grad_gate = summed[:, :hid][None]
    grad_up = summed[:, hid : 2 * hid][None]
    grad_down = summed[:, 2 * hid :][None]
    results = jnp.stack(
        [
            partial_out.reshape(parts, groups, CAP, feat),
            partial_grad.reshape(parts, groups, CAP, feat),
        ],
        axis=2,
    )
    returned = lax.all_to_all(
        results[0].astype(jnp.bfloat16), "expert", split_axis=0, concat_axis=0, tiled=True
    ).astype(jnp.float32)
    combined = jnp.sum(
        returned.reshape(window, SPLIT, 2, CAP, width), axis=1, keepdims=True
    ).astype(jnp.bfloat16)
    weighted = select * slot_gate[None, :, :]
    layer_out = jnp.einsum(
        "tec,ehcf->thf", weighted, combined[:, :, 0].astype(jnp.float32), precision=HIGH
    )
    token_grad = jnp.einsum(
        "tec,ehcf->thf", select, combined[:, :, 1].astype(jnp.float32), precision=HIGH
    )
    return (
        layer_out.reshape(tok_rows, width).astype(jnp.bfloat16),
        token_grad.reshape(tok_rows, width).astype(jnp.bfloat16),
        grad_gate,
        grad_up,
        grad_down,
    )


MESH = pl.DeviceIdType.MESH
F32 = jnp.float32
BF16 = jnp.bfloat16


def row_ids(shape):
    return lax.broadcasted_iota(jnp.int32, shape, 0)


def fold(v):
    half = v.shape[1] // 2
    return jnp.concatenate([v[:, :half], v[:, half:]], axis=0)


def unfold(v):
    rows = v.shape[0] // 2
    return jnp.concatenate([v[:rows], v[rows:]], axis=1)


def exchange_kernel(
    ids_hbm, gates_hbm, tok_hbm, cot_hbm, wg_hbm, wu_hbm, wd_hbm,
    gg_out, gu_out, gd_out, slot_out, sel_out,
    ids_v, gates_v, both_v, w_v, w_t, gath, rows_v, act_v, part, pex_s, pex_r, res, ra, sb, rb, sc, rc,
    across, mate_s, mate_r, grad_v, load_sem, send_sem, recv_sem,
):
    y = lax.axis_index("dp")
    e = lax.axis_index("expert")
    z, x, c = e // 4, (e // 2) % 2, e % 2

    def dev(zz, xx, cc):
        return zz * 4 + xx * 2 + cc

    def pos(zz, xx, cc):
        return (zz // 2) * 8 + cc * 4 + xx * 2 + zz % 2

    near = [z, z + 1 - 2 * (z % 2), (z + 2) % 4, 3 - z]
    peer_y = (1 - y, e)
    peer_c = (y, dev(z, x, 1 - c))
    peer_x = (y, dev(z, 1 - x, c))
    line = [[(yy, dev(zz, x, c)) for zz in near] for yy in (y, 1 - y)]

    started = []

    def remote(src, dst, target):
        n = len(started)
        copy = pltpu.make_async_remote_copy(
            src_ref=src, dst_ref=dst, send_sem=send_sem.at[n], recv_sem=recv_sem.at[n],
            device_id=target, device_id_type=MESH,
        )
        copy.start()
        started.append(copy)
        return copy

    n_tok = tok_hbm.shape[0]
    loads = [
        pltpu.make_async_copy(ids_hbm, ids_v, load_sem.at[0]),
        pltpu.make_async_copy(gates_hbm, gates_v, load_sem.at[1]),
        pltpu.make_async_copy(tok_hbm, both_v.at[:n_tok], load_sem.at[2]),
        pltpu.make_async_copy(cot_hbm, both_v.at[n_tok:], load_sem.at[3]),
        pltpu.make_async_copy(wg_hbm, w_v.at[:, 0:128], load_sem.at[4]),
        pltpu.make_async_copy(wu_hbm, w_v.at[:, 128:256], load_sem.at[5]),
        pltpu.make_async_copy(wd_hbm, w_v.at[:, 256:384], load_sem.at[6]),
    ]
    for load in loads:
        load.start()
    barrier = pltpu.get_barrier_semaphore()
    greeted = [peer_c, peer_x] + line[0][1:] + line[1]
    for target in greeted:
        pl.semaphore_signal(barrier, inc=1, device_id=target, device_id_type=MESH)

    square = (n_tok, n_tok)
    before = jnp.where(row_ids(square) < lax.broadcasted_iota(jnp.int32, square, 1), 1.0, 0.0).astype(BF16)
    loads[0].wait()
    loads[1].wait()
    hits = ids_v[...] == 0
    member = jnp.sum(jnp.where(hits, 1.0, 0.0), axis=0, keepdims=True)
    weight = jnp.sum(jnp.where(hits, gates_v[...].astype(F32), 0.0), axis=0, keepdims=True) * SCALE
    member8 = jnp.broadcast_to(member, (8, n_tok))
    rank = jnp.dot(member8.astype(BF16), before, preferred_element_type=F32)
    wanted = (row_ids((8, n_tok)) % CAP).astype(F32)
    sel = jnp.where(jnp.logical_and(rank == wanted, member8 > 0.5), 1.0, 0.0)
    sel_out[...] = sel
    gate8 = jnp.sum(sel * weight, axis=1, keepdims=True)
    nothing = jnp.zeros_like(sel)
    pick = jnp.concatenate(
        [jnp.concatenate([sel, nothing], axis=1), jnp.concatenate([nothing, sel], axis=1)], axis=0
    ).astype(BF16)
    loads[2].wait()
    loads[3].wait()
    slots = jnp.dot(pick, both_v[...], preferred_element_type=F32)
    half = slots.shape[1] // 2
    low = row_ids((8, half)) < 4
    piece_lo = jnp.where(low, slots[:8, :half], slots[8:, :half] * gate8)
    piece_hi = jnp.where(low, slots[:8, half:], slots[8:, half:] * gate8)
    here = pos(z, x, c)
    gath[here, y] = fold(jnp.where(y == 0, piece_lo, piece_hi)).astype(BF16)
    across[...] = fold(jnp.where(y == 0, piece_hi, piece_lo)).astype(BF16)
    pl.semaphore_wait(barrier, len(greeted))

    own = gath.at[here, y]
    over_z = [[None] * 4, [None] * 4]
    for k in (2, 1, 0):
        if k:
            over_z[0][k] = remote(own, own, line[0][k])
        over_z[1][k] = remote(across, own, line[1][k])
    over_x, over_c = [], [[], []]

    def forward(k):
        at = pos(near[k], x, c)
        for copy in (over_z[0][k], over_z[1][k]):
            if copy is not None:
                copy.wait_recv()
        if k == 2:
            over_z[0][3] = remote(gath.at[at], gath.at[at], line[0][1])
        over_x.append(remote(gath.at[at], gath.at[at], peer_x))
        over_c[k // 2].append(remote(gath.at[at], gath.at[at], peer_c))

    def forward_x(k):
        at = pos(near[k], 1 - x, c)
        over_x[k].wait_recv()
        over_c[k // 2].append(remote(gath.at[at], gath.at[at], peer_c))

    low3 = lax.broadcasted_iota(jnp.int32, (8, 8, 384), 1) < 4

    def project(h):
        for n in range(8):
            got = gath[h * 8 + n].astype(F32)
            rows_v[h * 8 + n] = jnp.concatenate([unfold(got[0]), unfold(got[1])], axis=0).astype(BF16)
        rows = rows_v[pl.ds(h * 8, 8)].reshape(128, half)
        p = jnp.dot(rows, w_v[...], preferred_element_type=F32).reshape(8, 2, 8, 384)
        p0, p1 = p[:, 0], p[:, 1]
        down1 = pltpu.roll(p1.reshape(64, 384), 4, 0).reshape(8, 8, 384)
        up0 = pltpu.roll(p0.reshape(64, 384), 60, 0).reshape(8, 8, 384)
        tok_part = jnp.where(low3, p0, down1)
        cot_part = jnp.where(low3, up0, p1)
        both = jnp.concatenate([tok_part[:, :, :256], cot_part[:, :, 256:]], axis=2).reshape(64, 384)
        part[h] = both
        pex_s[h] = both.astype(BF16)
        return remote(pex_s.at[h], pex_r.at[h], peer_y)

    def activate(h):
        total = part[h] + pex_r[h].astype(F32)
        gate_pre, up_pre, d_hidden = total[:, :128], total[:, 128:256], total[:, 256:]
        sig = jax.nn.sigmoid(gate_pre)
        act = gate_pre * sig
        hidden = (act * up_pre).astype(BF16)
        d_gate = (d_hidden * up_pre * sig * (1.0 + gate_pre * (1.0 - sig))).astype(BF16)
        d_up = (d_hidden * act).astype(BF16)
        d_both = jnp.concatenate([d_gate, d_up], axis=1)
        out = jnp.dot(hidden, w_t[256:], preferred_element_type=F32)
        grad = jnp.dot(d_both, w_t[:256], preferred_element_type=F32)
        res[pl.ds(h * 8, 8)] = jnp.concatenate(
            [out.reshape(8, 8, half), grad.reshape(8, 8, half)], axis=1
        ).astype(BF16)
        acts = jnp.concatenate([d_both, hidden], axis=1).astype(F32)
        up = pltpu.roll(acts, 60, 0).reshape(8, 8, 384)
        down = pltpu.roll(acts, 4, 0).reshape(8, 8, 384)
        acts = acts.reshape(8, 8, 384)
        for_tok = lax.broadcasted_iota(jnp.int32, (8, 8, 384), 2) < 256
        act_v[pl.ds(h * 8, 8)] = jnp.concatenate(
            [
                jnp.where(for_tok, jnp.where(low3, acts, 0.0), jnp.where(low3, 0.0, down)),
                jnp.where(for_tok, jnp.where(low3, up, 0.0), jnp.where(low3, 0.0, acts)),
            ],
            axis=1,
        ).astype(BF16)

    def core_chunks(part_of):
        for copy in over_c[part_of]:
            copy.wait_recv()

    def to_core(pair):
        src = res.at[pl.ds(pair * 8 + (1 - c) * 4, 4)]
        return remote(src, ra.at[pl.ds(pair * 4, 4)], peer_c)

    def core_sum(k, xx):
        zz = near[k]
        return res[pos(zz, xx, c)].astype(F32) + ra[(zz // 2) * 4 + xx * 2 + zz % 2].astype(F32)

    to_x = [None] * 4

    def send_x(k):
        sb[k] = core_sum(k, 1 - x).astype(BF16)
        to_x[k] = remote(sb.at[k], rb.at[k], peer_x)

    grad_copies = []

    def gradients(n):
        cols = half // 7
        rows = rows_v[:, :, n * cols : (n + 1) * cols].reshape(256, cols)
        tn = (((0,), (0,)), ((), ()))
        terms = lax.dot_general(rows, act_v[...].reshape(256, 384), tn, preferred_element_type=F32)
        for i, out in enumerate((gg_out, gu_out, gd_out)):
            at = pl.ds(n * cols, cols)
            grad_v[i, at] = terms[:, i * 128 : (i + 1) * 128]
            copy = pltpu.make_async_copy(grad_v.at[i, at], out.at[at], load_sem.at[7 + 3 * n + i])
            copy.start()
            grad_copies.append(copy)

    def summed(k):
        mid = core_sum(k, x)
        to_x[k].wait_recv()
        return mid + rb[k].astype(F32)

    def for_y(mid):
        out8, grad8 = mid[:8], mid[8:]
        for_0 = jnp.where(low, out8, pltpu.roll(grad8, 4, 0))
        for_1 = jnp.where(low, pltpu.roll(out8, 4, 0), grad8)
        return jnp.where(y == 0, for_0, for_1), jnp.where(y == 0, for_1, for_0)

    to_z = []

    def send_z(k, mid):
        same, other = for_y(mid)
        sc[1, k] = fold(other).astype(BF16)
        to_z.append((1, k, remote(sc.at[1, k], rc.at[1, k], line[1][k])))
        if k:
            sc[0, k] = fold(same).astype(BF16)
            to_z.append((0, k, remote(sc.at[0, k], rc.at[0, k], line[0][k])))
        return same

    def transposed(n):
        at = slice(n * 128, (n + 1) * 128)
        loads[4 + n].wait()
        w_t[at] = jnp.transpose(w_v[:, at])

    pair = z // 2
    transposed(2)
    forward(0)
    forward(1)
    forward_x(0)
    transposed(0)
    forward(2)
    forward_x(1)
    transposed(1)
    forward(3)
    core_chunks(0)
    swap_near = project(pair)
    forward_x(2)
    forward_x(3)
    core_chunks(1)
    swap_far = project(1 - pair)
    swap_near.wait_recv()
    activate(pair)
    core_near = to_core(pair)
    core_near.wait_recv()
    send_x(1)
    send_x(0)
    swap_far.wait_recv()
    activate(1 - pair)
    core_far = to_core(1 - pair)
    gradients(0)
    gradients(1)
    core_far.wait_recv()
    send_x(3)
    send_x(2)
    send_z(1, summed(1))
    same = send_z(0, summed(0))
    gradients(2)
    mate_s[...] = summed(3).astype(BF16)
    to_mate = remote(mate_s, mate_r, line[0][1])
    far = summed(2)
    gradients(3)
    to_mate.wait_recv()
    send_z(2, far + mate_r[...].astype(F32))
    for n in (4, 5, 6):
        gradients(n)
    total = [same, jnp.zeros_like(same)]
    for s_y, k, copy in to_z:
        copy.wait_recv()
        total[s_y] = total[s_y] + unfold(rc[s_y, k].astype(F32))
    mine8, got8 = (t.astype(BF16).astype(F32) for t in total)
    scale = jnp.where(row_ids((8, 1)) < 4, gate8, 1.0)
    slot_out[:, :half] = jnp.where(y == 0, mine8, got8) * scale
    slot_out[:, half:] = jnp.where(y == 0, got8, mine8) * scale
    for copy in grad_copies:
        copy.wait()
    for copy in started:
        copy.wait_send()


def output_kernel(slot_ref, sel_ref, gg_in, gu_in, gd_in, out_ref, tg_ref, gg_ref, gu_ref, gd_ref, rows, held, sems):
    copies = []

    def move(src, dst):
        copy = pltpu.make_async_copy(src, dst, sems.at[len(copies)])
        copy.start()
        copies.append(copy)
        return copy

    cut = gg_in.shape[0] // 2
    arriving = []
    for n in range(2):
        at = pl.ds(n * cut, cut)
        for i, (src, dst) in enumerate(((gg_in, gg_ref), (gu_in, gu_ref), (gd_in, gd_ref))):
            arriving.append((move(src.at[at], held.at[i, at]), held.at[i, at], dst.at[at]))
    sel = sel_ref[...]
    low = row_ids(sel.shape) < 4
    slots = slot_ref[...].astype(BF16)
    tn = (((0,), (0,)), ((), ()))
    for n, (ref, keep) in enumerate(((out_ref, low), (tg_ref, jnp.logical_not(low)))):
        picks = jnp.where(keep, sel, 0.0).astype(BF16)
        rows[n] = lax.dot_general(picks, slots, tn, preferred_element_type=F32).astype(BF16)
        move(rows.at[n], ref)
        for copy, src, dst in arriving[3 * n : 3 * n + 3]:
            copy.wait()
            move(src, dst)
    for copy in copies[6:]:
        copy.wait()


def per_device_fused(tokens, out_cotangent, expert_ids, gate_fixed, w_gate, w_up, w_down):
    n_tok, width = tokens.shape
    half = width // 2
    hbm = pl.BlockSpec(memory_space=pltpu.HBM)
    vmem = pl.BlockSpec(memory_space=pltpu.VMEM)
    copies = 35
    chunks = lambda n: pltpu.VMEM((n, 16, half), BF16)
    pieces = lambda m, n: pltpu.VMEM((m, n, 16, half // 2), BF16)
    gg, gu, gd, slots, sel = pl.pallas_call(
        exchange_kernel,
        out_shape=(
            *[jax.ShapeDtypeStruct((half, 128), F32)] * 3,
            jax.ShapeDtypeStruct((8, width), F32),
            jax.ShapeDtypeStruct((8, n_tok), F32),
        ),
        in_specs=[hbm] * 7,
        out_specs=(hbm, hbm, hbm, vmem, vmem),
        scratch_shapes=[
            pltpu.VMEM(expert_ids.shape[::-1], jnp.int32),
            pltpu.VMEM(gate_fixed.shape[::-1], jnp.int32),
            pltpu.VMEM((2 * n_tok, width), BF16),
            pltpu.VMEM((half, 384), BF16),
            pltpu.VMEM((384, half), BF16),
            pieces(16, 2),
            chunks(16),
            pltpu.VMEM((16, 16, 384), BF16),
            pltpu.VMEM((2, 64, 384), F32),
            pltpu.VMEM((2, 64, 384), BF16),
            pltpu.VMEM((2, 64, 384), BF16),
            chunks(16),
            chunks(8),
            chunks(4),
            chunks(4),
            pieces(2, 4),
            pieces(2, 4),
            pltpu.VMEM((16, half // 2), BF16),
            pltpu.VMEM((16, half), BF16),
            pltpu.VMEM((16, half), BF16),
            pltpu.VMEM((3, half, 128), F32),
            pltpu.SemaphoreType.DMA((28,)),
            pltpu.SemaphoreType.DMA((copies,)),
            pltpu.SemaphoreType.DMA((copies,)),
        ],
        compiler_params=pltpu.CompilerParams(
            collective_id=0, has_side_effects=True, vmem_limit_bytes=60 * 1024 * 1024
        ),
        cost_estimate=pl.CostEstimate(flops=400_000_000, bytes_accessed=6_000_000, transcendentals=16384),
        name="exchange",
    )(expert_ids.T, gate_fixed.T, tokens, out_cotangent, w_gate[0], w_up[0], w_down[0])
    layer_out, token_grad, gg, gu, gd = pl.pallas_call(
        output_kernel,
        out_shape=(jax.ShapeDtypeStruct((n_tok, width), BF16),) * 2
        + (jax.ShapeDtypeStruct((half, 128), F32),) * 3,
        in_specs=[vmem, vmem, hbm, hbm, hbm],
        out_specs=(hbm,) * 5,
        scratch_shapes=[
            pltpu.VMEM((2, n_tok, width), BF16),
            pltpu.VMEM((3, half, 128), F32),
            pltpu.SemaphoreType.DMA((14,)),
        ],
        compiler_params=pltpu.CompilerParams(vmem_limit_bytes=60 * 1024 * 1024),
        cost_estimate=pl.CostEstimate(flops=15_000_000, bytes_accessed=8_000_000, transcendentals=0),
        name="outputs",
    )(slots, sel, gg, gu, gd)
    return (layer_out, token_grad, gg[None], gu[None], gd[None])


def solution(mesh):
    sizes = (mesh.shape["dp"], mesh.shape["expert"])
    return jax.shard_map(
        per_device_fused if sizes == (2, 16) else per_device,
        mesh=mesh,
        in_specs=(
            P(("dp", "expert"), None),
            P(("dp", "expert"), None),
            P(("dp", "expert"), None),
            P(("dp", "expert"), None),
            P("expert", "dp", None),
            P("expert", "dp", None),
            P("expert", "dp", None),
        ),
        out_specs=(
            P(("dp", "expert"), None),
            P(("dp", "expert"), None),
            P("expert", "dp", None),
            P("expert", "dp", None),
            P("expert", "dp", None),
        ),
        check_vma=False,
    )
```

```python
import jax
import jax.numpy as jnp
from jax import lax
from jax.sharding import PartitionSpec as P
from jax.experimental import pallas as pl
from jax.experimental.pallas import tpu as pltpu

SPLIT = 16
CAP = 4


SCALE = 2.0 ** (-16)
HIGH = lax.Precision.HIGHEST


def routing(ids, gates, window, capacity):
    wanted = jnp.arange(window, dtype=jnp.int32)
    hits = ids[:, :, None] == wanted[None, None, :]
    member = jnp.any(hits, axis=1)
    weight = jnp.sum(jnp.where(hits, gates[:, :, None], 0), axis=1).astype(jnp.float32) * SCALE
    rank = jnp.cumsum(member.astype(jnp.int32), axis=0) - 1
    slots = jnp.arange(capacity, dtype=jnp.int32)
    pick = jnp.logical_and(member[:, :, None], rank[:, :, None] == slots[None, None, :])
    select = jnp.where(pick, 1.0, 0.0).astype(jnp.float32)
    slot_gate = jnp.sum(select * weight[:, :, None], axis=0)
    return (select, slot_gate)


def expert_math(inputs, cotangents, gate_w, up_w, down_w):
    gate_pre = jnp.einsum("prf,pfh->rh", inputs, gate_w, preferred_element_type=jnp.float32)
    up_pre = jnp.einsum("prf,pfh->rh", inputs, up_w, preferred_element_type=jnp.float32)
    sig = jax.nn.sigmoid(gate_pre)
    act = gate_pre * sig
    hidden = (act * up_pre).astype(jnp.bfloat16)
    partial_out = jnp.einsum("rh,pfh->prf", hidden, down_w, preferred_element_type=jnp.float32)
    d_hidden = jnp.einsum("prf,pfh->rh", cotangents, down_w, preferred_element_type=jnp.float32)
    d_gate = (d_hidden * up_pre * sig * (1.0 + gate_pre * (1.0 - sig))).astype(jnp.bfloat16)
    d_up = (d_hidden * act).astype(jnp.bfloat16)
    partial_grad = jnp.einsum(
        "rh,pfh->prf", d_gate, gate_w, preferred_element_type=jnp.float32
    ) + jnp.einsum("rh,pfh->prf", d_up, up_w, preferred_element_type=jnp.float32)
    term = jnp.concatenate(
        [
            jnp.einsum("prf,rh->pfh", inputs, d_gate, preferred_element_type=jnp.float32),
            jnp.einsum("prf,rh->pfh", inputs, d_up, preferred_element_type=jnp.float32),
            jnp.einsum("prf,rh->pfh", cotangents, hidden, preferred_element_type=jnp.float32),
        ],
        axis=2,
    )
    return (partial_out, partial_grad, term.reshape(-1, term.shape[2]))


def per_device(tokens, out_cotangent, expert_ids, gate_fixed, w_gate, w_up, w_down):
    tok_rows, width = tokens.shape
    groups = lax.axis_size("expert")
    window = groups // SPLIT
    hid = w_gate.shape[2]
    parts = 1
    feat = width // parts
    select, slot_gate = routing(expert_ids, gate_fixed, window, CAP)
    select_b = select.astype(jnp.bfloat16)
    tok3 = tokens.reshape(tok_rows, parts, feat)
    cot3 = out_cotangent.reshape(tok_rows, parts, feat)
    slot_tokens = jnp.einsum(
        "tec,tsf->escf", select_b, tok3, preferred_element_type=jnp.float32
    ).astype(jnp.bfloat16)
    picked = jnp.einsum("tec,tsf->escf", select_b, cot3, preferred_element_type=jnp.float32)
    slot_cot = (picked * slot_gate[:, None, :, None]).astype(jnp.bfloat16)
    payload = jnp.stack([slot_tokens, slot_cot], axis=2)
    gate_full, up_full, down_full = (
        lax.all_gather(w_gate, "dp", axis=1, tiled=True),
        lax.all_gather(w_up, "dp", axis=1, tiled=True),
        lax.all_gather(w_down, "dp", axis=1, tiled=True),
    )
    outgoing = jnp.broadcast_to(payload, (window, SPLIT, 2, CAP, width)).reshape(
        groups, 2, CAP, width
    )
    arrived = lax.all_to_all(outgoing, "expert", split_axis=0, concat_axis=0, tiled=True)
    pieces = arrived[None]
    inputs = pieces[:, :, 0].reshape(parts, groups * CAP, feat)
    cotangents = pieces[:, :, 1].reshape(parts, groups * CAP, feat)
    partial_out, partial_grad, term = expert_math(inputs, cotangents, gate_full, up_full, down_full)
    summed = lax.psum_scatter(
        term.astype(jnp.bfloat16), "dp", scatter_dimension=0, tiled=True
    ).astype(jnp.float32)
    grad_gate = summed[:, :hid][None]
    grad_up = summed[:, hid : 2 * hid][None]
    grad_down = summed[:, 2 * hid :][None]
    results = jnp.stack(
        [
            partial_out.reshape(parts, groups, CAP, feat),
            partial_grad.reshape(parts, groups, CAP, feat),
        ],
        axis=2,
    )
    returned = lax.all_to_all(
        results[0].astype(jnp.bfloat16), "expert", split_axis=0, concat_axis=0, tiled=True
    ).astype(jnp.float32)
    combined = jnp.sum(
        returned.reshape(window, SPLIT, 2, CAP, width), axis=1, keepdims=True
    ).astype(jnp.bfloat16)
    weighted = select * slot_gate[None, :, :]
    layer_out = jnp.einsum(
        "tec,ehcf->thf", weighted, combined[:, :, 0].astype(jnp.float32), precision=HIGH
    )
    token_grad = jnp.einsum(
        "tec,ehcf->thf", select, combined[:, :, 1].astype(jnp.float32), precision=HIGH
    )
    return (
        layer_out.reshape(tok_rows, width).astype(jnp.bfloat16),
        token_grad.reshape(tok_rows, width).astype(jnp.bfloat16),
        grad_gate,
        grad_up,
        grad_down,
    )


MESH = pl.DeviceIdType.MESH
F32 = jnp.float32
BF16 = jnp.bfloat16


def row_ids(shape):
    return lax.broadcasted_iota(jnp.int32, shape, 0)


def fold(v):
    half = v.shape[1] // 2
    return jnp.concatenate([v[:, :half], v[:, half:]], axis=0)


def unfold(v):
    rows = v.shape[0] // 2
    return jnp.concatenate([v[:rows], v[rows:]], axis=1)


def exchange_kernel(
    ids_hbm, gates_hbm, tok_hbm, cot_hbm, wg_hbm, wu_hbm, wd_hbm,
    x_out, act_out, slot_out, sel_out,
    ids_v, gates_v, both_v, w_v, w_t, gath, rows_v, act_v, part, pex_s, pex_r, res, ra, sb, rb, sc, rc,
    across, mate_s, mate_r, load_sem, send_sem, recv_sem,
):
    y = lax.axis_index("dp")
    e = lax.axis_index("expert")
    z, x, c = e // 4, (e // 2) % 2, e % 2

    def dev(zz, xx, cc):
        return zz * 4 + xx * 2 + cc

    def pos(zz, xx, cc):
        return (zz // 2) * 8 + cc * 4 + xx * 2 + zz % 2

    near = [z, z + 1 - 2 * (z % 2), (z + 2) % 4, 3 - z]
    peer_y = (1 - y, e)
    peer_c = (y, dev(z, x, 1 - c))
    peer_x = (y, dev(z, 1 - x, c))
    line = [[(yy, dev(zz, x, c)) for zz in near] for yy in (y, 1 - y)]

    started = []

    def remote(src, dst, target):
        n = len(started)
        copy = pltpu.make_async_remote_copy(
            src_ref=src, dst_ref=dst, send_sem=send_sem.at[n], recv_sem=recv_sem.at[n],
            device_id=target, device_id_type=MESH,
        )
        copy.start()
        started.append(copy)
        return copy

    n_tok = tok_hbm.shape[0]
    loads = [
        pltpu.make_async_copy(ids_hbm, ids_v, load_sem.at[0]),
        pltpu.make_async_copy(gates_hbm, gates_v, load_sem.at[1]),
        pltpu.make_async_copy(tok_hbm, both_v.at[:n_tok], load_sem.at[2]),
        pltpu.make_async_copy(cot_hbm, both_v.at[n_tok:], load_sem.at[3]),
        pltpu.make_async_copy(wg_hbm, w_v.at[:, 0:128], load_sem.at[4]),
        pltpu.make_async_copy(wu_hbm, w_v.at[:, 128:256], load_sem.at[5]),
        pltpu.make_async_copy(wd_hbm, w_v.at[:, 256:384], load_sem.at[6]),
    ]
    for load in loads:
        load.start()
    barrier = pltpu.get_barrier_semaphore()
    greeted = [peer_c, peer_x] + line[0][1:] + line[1]
    for target in greeted:
        pl.semaphore_signal(barrier, inc=1, device_id=target, device_id_type=MESH)

    square = (n_tok, n_tok)
    before = jnp.where(row_ids(square) < lax.broadcasted_iota(jnp.int32, square, 1), 1.0, 0.0).astype(BF16)
    loads[0].wait()
    loads[1].wait()
    hits = ids_v[...] == 0
    member = jnp.sum(jnp.where(hits, 1.0, 0.0), axis=0, keepdims=True)
    weight = jnp.sum(jnp.where(hits, gates_v[...].astype(F32), 0.0), axis=0, keepdims=True) * SCALE
    member8 = jnp.broadcast_to(member, (8, n_tok))
    rank = jnp.dot(member8.astype(BF16), before, preferred_element_type=F32)
    wanted = (row_ids((8, n_tok)) % CAP).astype(F32)
    sel = jnp.where(jnp.logical_and(rank == wanted, member8 > 0.5), 1.0, 0.0)
    sel_out[...] = sel
    gate8 = jnp.sum(sel * weight, axis=1, keepdims=True)
    nothing = jnp.zeros_like(sel)
    pick = jnp.concatenate(
        [jnp.concatenate([sel, nothing], axis=1), jnp.concatenate([nothing, sel], axis=1)], axis=0
    ).astype(BF16)
    loads[2].wait()
    loads[3].wait()
    slots = jnp.dot(pick, both_v[...], preferred_element_type=F32)
    half = slots.shape[1] // 2
    low = row_ids((8, half)) < 4
    piece_lo = jnp.where(low, slots[:8, :half], slots[8:, :half] * gate8)
    piece_hi = jnp.where(low, slots[:8, half:], slots[8:, half:] * gate8)
    here = pos(z, x, c)
    gath[here, y] = fold(jnp.where(y == 0, piece_lo, piece_hi)).astype(BF16)
    across[...] = fold(jnp.where(y == 0, piece_hi, piece_lo)).astype(BF16)
    pl.semaphore_wait(barrier, len(greeted))

    own = gath.at[here, y]
    over_z = [[None] * 4, [None] * 4]
    for k in (2, 1, 0):
        if k:
            over_z[0][k] = remote(own, own, line[0][k])
        over_z[1][k] = remote(across, own, line[1][k])
    over_x, over_c = [], [[], []]

    def forward(k):
        at = pos(near[k], x, c)
        for copy in (over_z[0][k], over_z[1][k]):
            if copy is not None:
                copy.wait_recv()
        if k == 2:
            over_z[0][3] = remote(gath.at[at], gath.at[at], line[0][1])
        over_x.append(remote(gath.at[at], gath.at[at], peer_x))
        over_c[k // 2].append(remote(gath.at[at], gath.at[at], peer_c))

    def forward_x(k):
        at = pos(near[k], 1 - x, c)
        over_x[k].wait_recv()
        over_c[k // 2].append(remote(gath.at[at], gath.at[at], peer_c))

    low3 = lax.broadcasted_iota(jnp.int32, (8, 8, 384), 1) < 4

    def project(h):
        for n in range(8):
            got = gath[h * 8 + n].astype(F32)
            rows_v[h * 8 + n] = jnp.concatenate([unfold(got[0]), unfold(got[1])], axis=0).astype(BF16)
        rows = rows_v[pl.ds(h * 8, 8)].reshape(128, half)
        p = jnp.dot(rows, w_v[...], preferred_element_type=F32).reshape(8, 2, 8, 384)
        p0, p1 = p[:, 0], p[:, 1]
        down1 = pltpu.roll(p1.reshape(64, 384), 4, 0).reshape(8, 8, 384)
        up0 = pltpu.roll(p0.reshape(64, 384), 60, 0).reshape(8, 8, 384)
        tok_part = jnp.where(low3, p0, down1)
        cot_part = jnp.where(low3, up0, p1)
        both = jnp.concatenate([tok_part[:, :, :256], cot_part[:, :, 256:]], axis=2).reshape(64, 384)
        part[h] = both
        pex_s[h] = both.astype(BF16)
        return remote(pex_s.at[h], pex_r.at[h], peer_y)

    def activate(h):
        total = part[h] + pex_r[h].astype(F32)
        gate_pre, up_pre, d_hidden = total[:, :128], total[:, 128:256], total[:, 256:]
        sig = jax.nn.sigmoid(gate_pre)
        act = gate_pre * sig
        hidden = (act * up_pre).astype(BF16)
        d_gate = (d_hidden * up_pre * sig * (1.0 + gate_pre * (1.0 - sig))).astype(BF16)
        d_up = (d_hidden * act).astype(BF16)
        d_both = jnp.concatenate([d_gate, d_up], axis=1)
        out = jnp.dot(hidden, w_t[256:], preferred_element_type=F32)
        grad = jnp.dot(d_both, w_t[:256], preferred_element_type=F32)
        res[pl.ds(h * 8, 8)] = jnp.concatenate(
            [out.reshape(8, 8, half), grad.reshape(8, 8, half)], axis=1
        ).astype(BF16)
        acts = jnp.concatenate([d_both, hidden], axis=1).astype(F32)
        up = pltpu.roll(acts, 60, 0).reshape(8, 8, 384)
        down = pltpu.roll(acts, 4, 0).reshape(8, 8, 384)
        acts = acts.reshape(8, 8, 384)
        for_tok = lax.broadcasted_iota(jnp.int32, (8, 8, 384), 2) < 256
        act_v[pl.ds(h * 8, 8)] = jnp.concatenate(
            [
                jnp.where(for_tok, jnp.where(low3, acts, 0.0), jnp.where(low3, 0.0, down)),
                jnp.where(for_tok, jnp.where(low3, up, 0.0), jnp.where(low3, 0.0, acts)),
            ],
            axis=1,
        ).astype(BF16)

    def core_chunks(part_of):
        for copy in over_c[part_of]:
            copy.wait_recv()

    def to_core(pair):
        src = res.at[pl.ds(pair * 8 + (1 - c) * 4, 4)]
        return remote(src, ra.at[pl.ds(pair * 4, 4)], peer_c)

    def core_sum(k, xx):
        zz = near[k]
        return res[pos(zz, xx, c)].astype(F32) + ra[(zz // 2) * 4 + xx * 2 + zz % 2].astype(F32)

    to_x = [None] * 4

    def send_x(k):
        sb[k] = core_sum(k, 1 - x).astype(BF16)
        to_x[k] = remote(sb.at[k], rb.at[k], peer_x)

    def summed(k):
        mid = core_sum(k, x)
        to_x[k].wait_recv()
        return mid + rb[k].astype(F32)

    def for_y(mid):
        out8, grad8 = mid[:8], mid[8:]
        for_0 = jnp.where(low, out8, pltpu.roll(grad8, 4, 0))
        for_1 = jnp.where(low, pltpu.roll(out8, 4, 0), grad8)
        return jnp.where(y == 0, for_0, for_1), jnp.where(y == 0, for_1, for_0)

    to_z = []

    def send_z(k, mid):
        same, other = for_y(mid)
        sc[1, k] = fold(other).astype(BF16)
        to_z.append((1, k, remote(sc.at[1, k], rc.at[1, k], line[1][k])))
        if k:
            sc[0, k] = fold(same).astype(BF16)
            to_z.append((0, k, remote(sc.at[0, k], rc.at[0, k], line[0][k])))
        return same

    def transposed(n):
        at = slice(n * 128, (n + 1) * 128)
        loads[4 + n].wait()
        w_t[at] = jnp.transpose(w_v[:, at])

    pair = z // 2
    transposed(2)
    forward(0)
    forward(1)
    forward_x(0)
    transposed(0)
    forward(2)
    forward_x(1)
    transposed(1)
    forward(3)
    core_chunks(0)
    swap_near = project(pair)
    forward_x(2)
    forward_x(3)
    core_chunks(1)
    swap_far = project(1 - pair)
    keep_x = pltpu.make_async_copy(rows_v, x_out, load_sem.at[7])
    keep_x.start()
    swap_near.wait_recv()
    activate(pair)
    core_near = to_core(pair)
    core_near.wait_recv()
    send_x(1)
    send_x(0)
    swap_far.wait_recv()
    activate(1 - pair)
    core_far = to_core(1 - pair)
    keep_act = pltpu.make_async_copy(act_v, act_out, load_sem.at[8])
    keep_act.start()
    core_far.wait_recv()
    send_x(3)
    send_x(2)
    send_z(1, summed(1))
    same = send_z(0, summed(0))
    mate_s[...] = summed(3).astype(BF16)
    to_mate = remote(mate_s, mate_r, line[0][1])
    far = summed(2)
    to_mate.wait_recv()
    send_z(2, far + mate_r[...].astype(F32))
    total = [same, jnp.zeros_like(same)]
    for s_y, k, copy in to_z:
        copy.wait_recv()
        total[s_y] = total[s_y] + unfold(rc[s_y, k].astype(F32))
    mine8, got8 = (t.astype(BF16).astype(F32) for t in total)
    scale = jnp.where(row_ids((8, 1)) < 4, gate8, 1.0)
    slot_out[:, :half] = jnp.where(y == 0, mine8, got8) * scale
    slot_out[:, half:] = jnp.where(y == 0, got8, mine8) * scale
    keep_x.wait()
    keep_act.wait()
    for copy in started:
        copy.wait_send()


def output_kernel(x_ref, act_ref, slot_ref, sel_ref, out_ref, tg_ref, gg_ref, gu_ref, gd_ref):
    sel = sel_ref[...]
    low = row_ids(sel.shape) < 4
    slots = slot_ref[...].astype(BF16)
    tn = (((0,), (0,)), ((), ()))
    for ref, keep in ((out_ref, low), (tg_ref, jnp.logical_not(low))):
        picks = jnp.where(keep, sel, 0.0).astype(BF16)
        ref[...] = lax.dot_general(picks, slots, tn, preferred_element_type=F32).astype(BF16)
    grads = lax.dot_general(x_ref[...], act_ref[...], tn, preferred_element_type=F32)
    for n, ref in enumerate((gg_ref, gu_ref, gd_ref)):
        ref[...] = grads[:, n * 128 : (n + 1) * 128]


def per_device_fused(tokens, out_cotangent, expert_ids, gate_fixed, w_gate, w_up, w_down):
    n_tok, width = tokens.shape
    half = width // 2
    hbm = pl.BlockSpec(memory_space=pltpu.HBM)
    vmem = pl.BlockSpec(memory_space=pltpu.VMEM)
    copies = 35
    chunks = lambda n: pltpu.VMEM((n, 16, half), BF16)
    pieces = lambda m, n: pltpu.VMEM((m, n, 16, half // 2), BF16)
    x_all, act, slots, sel = pl.pallas_call(
        exchange_kernel,
        out_shape=(
            pltpu.VMEM((16, 16, half), BF16),
            pltpu.VMEM((16, 16, 384), BF16),
            pltpu.VMEM((8, width), F32),
            pltpu.VMEM((8, n_tok), F32),
        ),
        in_specs=[hbm] * 7,
        out_specs=(vmem,) * 4,
        scratch_shapes=[
            pltpu.VMEM(expert_ids.shape[::-1], jnp.int32),
            pltpu.VMEM(gate_fixed.shape[::-1], jnp.int32),
            pltpu.VMEM((2 * n_tok, width), BF16),
            pltpu.VMEM((half, 384), BF16),
            pltpu.VMEM((384, half), BF16),
            pieces(16, 2),
            chunks(16),
            pltpu.VMEM((16, 16, 384), BF16),
            pltpu.VMEM((2, 64, 384), F32),
            pltpu.VMEM((2, 64, 384), BF16),
            pltpu.VMEM((2, 64, 384), BF16),
            chunks(16),
            chunks(8),
            chunks(4),
            chunks(4),
            pieces(2, 4),
            pieces(2, 4),
            pltpu.VMEM((16, half // 2), BF16),
            pltpu.VMEM((16, half), BF16),
            pltpu.VMEM((16, half), BF16),
            pltpu.SemaphoreType.DMA((9,)),
            pltpu.SemaphoreType.DMA((copies,)),
            pltpu.SemaphoreType.DMA((copies,)),
        ],
        compiler_params=pltpu.CompilerParams(
            collective_id=0, has_side_effects=True, vmem_limit_bytes=60 * 1024 * 1024
        ),
        cost_estimate=pl.CostEstimate(flops=400_000_000, bytes_accessed=6_000_000, transcendentals=16384),
        name="exchange",
    )(expert_ids.T, gate_fixed.T, tokens, out_cotangent, w_gate[0], w_up[0], w_down[0])
    steps = 2
    grad_spec = pl.BlockSpec((half // steps, 128), lambda i: (i, 0))
    tok_spec = pl.BlockSpec((n_tok, width // steps), lambda i: (0, i))
    layer_out, token_grad, gg, gu, gd = pl.pallas_call(
        output_kernel,
        grid=(steps,),
        out_shape=(jax.ShapeDtypeStruct((n_tok, width), BF16),) * 2
        + (jax.ShapeDtypeStruct((half, 128), F32),) * 3,
        in_specs=[
            pl.BlockSpec((256, half // steps), lambda i: (0, i)),
            pl.BlockSpec((256, 384), lambda i: (0, 0)),
            pl.BlockSpec((8, width // steps), lambda i: (0, i)),
            pl.BlockSpec((8, n_tok), lambda i: (0, 0)),
        ],
        out_specs=(tok_spec, tok_spec, grad_spec, grad_spec, grad_spec),
        compiler_params=pltpu.CompilerParams(vmem_limit_bytes=32 * 1024 * 1024),
        cost_estimate=pl.CostEstimate(flops=400_000_000, bytes_accessed=6_000_000, transcendentals=0),
        name="outputs",
    )(x_all.reshape(256, half), act.reshape(256, 384), slots, sel)
    return (layer_out, token_grad, gg[None], gu[None], gd[None])


def solution(mesh):
    sizes = (mesh.shape["dp"], mesh.shape["expert"])
    return jax.shard_map(
        per_device_fused if sizes == (2, 16) else per_device,
        mesh=mesh,
        in_specs=(
            P(("dp", "expert"), None),
            P(("dp", "expert"), None),
            P(("dp", "expert"), None),
            P(("dp", "expert"), None),
            P("expert", "dp", None),
            P("expert", "dp", None),
            P("expert", "dp", None),
        ),
        out_specs=(
            P(("dp", "expert"), None),
            P(("dp", "expert"), None),
            P("expert", "dp", None),
            P("expert", "dp", None),
            P("expert", "dp", None),
        ),
        check_vma=False,
    )
```

```python
import jax
import jax.numpy as jnp
from jax import lax
from jax.sharding import PartitionSpec as P
from jax.experimental import pallas as pl
from jax.experimental.pallas import tpu as pltpu

SPLIT = 16
CAP = 4


SCALE = 2.0 ** (-16)
HIGH = lax.Precision.HIGHEST


def routing(ids, gates, window, capacity):
    wanted = jnp.arange(window, dtype=jnp.int32)
    hits = ids[:, :, None] == wanted[None, None, :]
    member = jnp.any(hits, axis=1)
    weight = jnp.sum(jnp.where(hits, gates[:, :, None], 0), axis=1).astype(jnp.float32) * SCALE
    rank = jnp.cumsum(member.astype(jnp.int32), axis=0) - 1
    slots = jnp.arange(capacity, dtype=jnp.int32)
    pick = jnp.logical_and(member[:, :, None], rank[:, :, None] == slots[None, None, :])
    select = jnp.where(pick, 1.0, 0.0).astype(jnp.float32)
    slot_gate = jnp.sum(select * weight[:, :, None], axis=0)
    return (select, slot_gate)


def expert_math(inputs, cotangents, gate_w, up_w, down_w):
    gate_pre = jnp.einsum("prf,pfh->rh", inputs, gate_w, preferred_element_type=jnp.float32)
    up_pre = jnp.einsum("prf,pfh->rh", inputs, up_w, preferred_element_type=jnp.float32)
    sig = jax.nn.sigmoid(gate_pre)
    act = gate_pre * sig
    hidden = (act * up_pre).astype(jnp.bfloat16)
    partial_out = jnp.einsum("rh,pfh->prf", hidden, down_w, preferred_element_type=jnp.float32)
    d_hidden = jnp.einsum("prf,pfh->rh", cotangents, down_w, preferred_element_type=jnp.float32)
    d_gate = (d_hidden * up_pre * sig * (1.0 + gate_pre * (1.0 - sig))).astype(jnp.bfloat16)
    d_up = (d_hidden * act).astype(jnp.bfloat16)
    partial_grad = jnp.einsum(
        "rh,pfh->prf", d_gate, gate_w, preferred_element_type=jnp.float32
    ) + jnp.einsum("rh,pfh->prf", d_up, up_w, preferred_element_type=jnp.float32)
    term = jnp.concatenate(
        [
            jnp.einsum("prf,rh->pfh", inputs, d_gate, preferred_element_type=jnp.float32),
            jnp.einsum("prf,rh->pfh", inputs, d_up, preferred_element_type=jnp.float32),
            jnp.einsum("prf,rh->pfh", cotangents, hidden, preferred_element_type=jnp.float32),
        ],
        axis=2,
    )
    return (partial_out, partial_grad, term.reshape(-1, term.shape[2]))


def per_device(tokens, out_cotangent, expert_ids, gate_fixed, w_gate, w_up, w_down):
    tok_rows, width = tokens.shape
    groups = lax.axis_size("expert")
    window = groups // SPLIT
    hid = w_gate.shape[2]
    parts = 1
    feat = width // parts
    select, slot_gate = routing(expert_ids, gate_fixed, window, CAP)
    select_b = select.astype(jnp.bfloat16)
    tok3 = tokens.reshape(tok_rows, parts, feat)
    cot3 = out_cotangent.reshape(tok_rows, parts, feat)
    slot_tokens = jnp.einsum(
        "tec,tsf->escf", select_b, tok3, preferred_element_type=jnp.float32
    ).astype(jnp.bfloat16)
    picked = jnp.einsum("tec,tsf->escf", select_b, cot3, preferred_element_type=jnp.float32)
    slot_cot = (picked * slot_gate[:, None, :, None]).astype(jnp.bfloat16)
    payload = jnp.stack([slot_tokens, slot_cot], axis=2)
    gate_full, up_full, down_full = (
        lax.all_gather(w_gate, "dp", axis=1, tiled=True),
        lax.all_gather(w_up, "dp", axis=1, tiled=True),
        lax.all_gather(w_down, "dp", axis=1, tiled=True),
    )
    outgoing = jnp.broadcast_to(payload, (window, SPLIT, 2, CAP, width)).reshape(
        groups, 2, CAP, width
    )
    arrived = lax.all_to_all(outgoing, "expert", split_axis=0, concat_axis=0, tiled=True)
    pieces = arrived[None]
    inputs = pieces[:, :, 0].reshape(parts, groups * CAP, feat)
    cotangents = pieces[:, :, 1].reshape(parts, groups * CAP, feat)
    partial_out, partial_grad, term = expert_math(inputs, cotangents, gate_full, up_full, down_full)
    summed = lax.psum_scatter(
        term.astype(jnp.bfloat16), "dp", scatter_dimension=0, tiled=True
    ).astype(jnp.float32)
    grad_gate = summed[:, :hid][None]
    grad_up = summed[:, hid : 2 * hid][None]
    grad_down = summed[:, 2 * hid :][None]
    results = jnp.stack(
        [
            partial_out.reshape(parts, groups, CAP, feat),
            partial_grad.reshape(parts, groups, CAP, feat),
        ],
        axis=2,
    )
    returned = lax.all_to_all(
        results[0].astype(jnp.bfloat16), "expert", split_axis=0, concat_axis=0, tiled=True
    ).astype(jnp.float32)
    combined = jnp.sum(
        returned.reshape(window, SPLIT, 2, CAP, width), axis=1, keepdims=True
    ).astype(jnp.bfloat16)
    weighted = select * slot_gate[None, :, :]
    layer_out = jnp.einsum(
        "tec,ehcf->thf", weighted, combined[:, :, 0].astype(jnp.float32), precision=HIGH
    )
    token_grad = jnp.einsum(
        "tec,ehcf->thf", select, combined[:, :, 1].astype(jnp.float32), precision=HIGH
    )
    return (
        layer_out.reshape(tok_rows, width).astype(jnp.bfloat16),
        token_grad.reshape(tok_rows, width).astype(jnp.bfloat16),
        grad_gate,
        grad_up,
        grad_down,
    )


MESH = pl.DeviceIdType.MESH
F32 = jnp.float32
BF16 = jnp.bfloat16


def row_ids(shape):
    return lax.broadcasted_iota(jnp.int32, shape, 0)


def fold(v):
    half = v.shape[1] // 2
    return jnp.concatenate([v[:, :half], v[:, half:]], axis=0)


def unfold(v):
    rows = v.shape[0] // 2
    return jnp.concatenate([v[:rows], v[rows:]], axis=1)


def exchange_kernel(
    ids_hbm, gates_hbm, tok_hbm, cot_hbm, wg_hbm, wu_hbm, wd_hbm,
    x_out, act_out, slot_out, sel_out,
    ids_v, gates_v, both_v, w_v, w_t, gath, rows_v, act_v, part, pex_s, pex_r, res, ra, sb, rb, sc, rc,
    across, load_sem, send_sem, recv_sem,
):
    y = lax.axis_index("dp")
    e = lax.axis_index("expert")
    z, x, c = e // 4, (e // 2) % 2, e % 2

    def dev(zz, xx, cc):
        return zz * 4 + xx * 2 + cc

    def pos(zz, xx, cc):
        return cc * 8 + xx * 4 + zz

    near = [z, z + 1 - 2 * (z % 2), (z + 2) % 4, 3 - z]
    peer_y = (1 - y, e)
    peer_c = (y, dev(z, x, 1 - c))
    peer_x = (y, dev(z, 1 - x, c))
    line = [[(yy, dev(zz, x, c)) for zz in near] for yy in (y, 1 - y)]

    started = []

    def remote(src, dst, target):
        n = len(started)
        copy = pltpu.make_async_remote_copy(
            src_ref=src, dst_ref=dst, send_sem=send_sem.at[n], recv_sem=recv_sem.at[n],
            device_id=target, device_id_type=MESH,
        )
        copy.start()
        started.append(copy)
        return copy

    n_tok = tok_hbm.shape[0]
    loads = [
        pltpu.make_async_copy(ids_hbm, ids_v, load_sem.at[0]),
        pltpu.make_async_copy(gates_hbm, gates_v, load_sem.at[1]),
        pltpu.make_async_copy(tok_hbm, both_v.at[:n_tok], load_sem.at[2]),
        pltpu.make_async_copy(cot_hbm, both_v.at[n_tok:], load_sem.at[3]),
        pltpu.make_async_copy(wg_hbm, w_v.at[:, 0:128], load_sem.at[4]),
        pltpu.make_async_copy(wu_hbm, w_v.at[:, 128:256], load_sem.at[5]),
        pltpu.make_async_copy(wd_hbm, w_v.at[:, 256:384], load_sem.at[6]),
    ]
    for load in loads:
        load.start()
    barrier = pltpu.get_barrier_semaphore()
    greeted = [peer_c, peer_x] + line[0][1:] + line[1]
    for target in greeted:
        pl.semaphore_signal(barrier, inc=1, device_id=target, device_id_type=MESH)

    square = (n_tok, n_tok)
    before = jnp.where(row_ids(square) < lax.broadcasted_iota(jnp.int32, square, 1), 1.0, 0.0).astype(BF16)
    loads[0].wait()
    loads[1].wait()
    hits = ids_v[...] == 0
    member = jnp.sum(jnp.where(hits, 1.0, 0.0), axis=0, keepdims=True)
    weight = jnp.sum(jnp.where(hits, gates_v[...].astype(F32), 0.0), axis=0, keepdims=True) * SCALE
    member8 = jnp.broadcast_to(member, (8, n_tok))
    rank = jnp.dot(member8.astype(BF16), before, preferred_element_type=F32)
    wanted = (row_ids((8, n_tok)) % CAP).astype(F32)
    sel = jnp.where(jnp.logical_and(rank == wanted, member8 > 0.5), 1.0, 0.0)
    sel_out[...] = sel
    gate8 = jnp.sum(sel * weight, axis=1, keepdims=True)
    nothing = jnp.zeros_like(sel)
    pick = jnp.concatenate(
        [jnp.concatenate([sel, nothing], axis=1), jnp.concatenate([nothing, sel], axis=1)], axis=0
    ).astype(BF16)
    loads[2].wait()
    loads[3].wait()
    slots = jnp.dot(pick, both_v[...], preferred_element_type=F32)
    half = slots.shape[1] // 2
    low = row_ids((8, half)) < 4
    piece_lo = jnp.where(low, slots[:8, :half], slots[8:, :half] * gate8)
    piece_hi = jnp.where(low, slots[:8, half:], slots[8:, half:] * gate8)
    here = pos(z, x, c)
    gath[here, y] = fold(jnp.where(y == 0, piece_lo, piece_hi)).astype(BF16)
    across[...] = fold(jnp.where(y == 0, piece_hi, piece_lo)).astype(BF16)
    pl.semaphore_wait(barrier, len(greeted))

    own = gath.at[here, y]
    over_z = [[None] * 4, [None] * 4]
    over_z[1][0] = remote(across, own, line[1][0])
    for k in (1, 2, 3):
        over_z[0][k] = remote(own, own, line[0][k])
        over_z[1][k] = remote(across, own, line[1][k])
    over_x, over_c = [], []
    for k in range(4):
        at = pos(near[k], x, c)
        for copy in (over_z[0][k], over_z[1][k]):
            if copy is not None:
                copy.wait_recv()
        over_x.append(remote(gath.at[at], gath.at[at], peer_x))
        over_c.append(remote(gath.at[at], gath.at[at], peer_c))
    for k in range(4):
        at = pos(near[k], 1 - x, c)
        over_x[k].wait_recv()
        over_c.append(remote(gath.at[at], gath.at[at], peer_c))

    for load in loads[4:]:
        load.wait()

    low3 = lax.broadcasted_iota(jnp.int32, (8, 8, 384), 1) < 4

    def project(h):
        for n in range(8):
            got = gath[h * 8 + n].astype(F32)
            rows_v[h * 8 + n] = jnp.concatenate([unfold(got[0]), unfold(got[1])], axis=0).astype(BF16)
        rows = rows_v[pl.ds(h * 8, 8)].reshape(128, half)
        p = jnp.dot(rows, w_v[...], preferred_element_type=F32).reshape(8, 2, 8, 384)
        p0, p1 = p[:, 0], p[:, 1]
        down1 = pltpu.roll(p1.reshape(64, 384), 4, 0).reshape(8, 8, 384)
        up0 = pltpu.roll(p0.reshape(64, 384), 60, 0).reshape(8, 8, 384)
        tok_part = jnp.where(low3, p0, down1)
        cot_part = jnp.where(low3, up0, p1)
        both = jnp.concatenate([tok_part[:, :, :256], cot_part[:, :, 256:]], axis=2).reshape(64, 384)
        part[h] = both
        pex_s[h] = both.astype(BF16)
        return remote(pex_s.at[h], pex_r.at[h], peer_y)

    def activate(h):
        total = part[h] + pex_r[h].astype(F32)
        gate_pre, up_pre, d_hidden = total[:, :128], total[:, 128:256], total[:, 256:]
        sig = jax.nn.sigmoid(gate_pre)
        act = gate_pre * sig
        hidden = (act * up_pre).astype(BF16)
        d_gate = (d_hidden * up_pre * sig * (1.0 + gate_pre * (1.0 - sig))).astype(BF16)
        d_up = (d_hidden * act).astype(BF16)
        d_both = jnp.concatenate([d_gate, d_up], axis=1)
        out = jnp.dot(hidden, w_t[256:], preferred_element_type=F32)
        grad = jnp.dot(d_both, w_t[:256], preferred_element_type=F32)
        res[pl.ds(h * 8, 8)] = jnp.concatenate(
            [out.reshape(8, 8, half), grad.reshape(8, 8, half)], axis=1
        ).astype(BF16)
        acts = jnp.concatenate([d_both, hidden], axis=1).astype(F32)
        up = pltpu.roll(acts, 60, 0).reshape(8, 8, 384)
        down = pltpu.roll(acts, 4, 0).reshape(8, 8, 384)
        acts = acts.reshape(8, 8, 384)
        for_tok = lax.broadcasted_iota(jnp.int32, (8, 8, 384), 2) < 256
        act_v[pl.ds(h * 8, 8)] = jnp.concatenate(
            [
                jnp.where(for_tok, jnp.where(low3, acts, 0.0), jnp.where(low3, 0.0, down)),
                jnp.where(for_tok, jnp.where(low3, up, 0.0), jnp.where(low3, 0.0, acts)),
            ],
            axis=1,
        ).astype(BF16)

    swap_own = project(c)
    for copy in over_c:
        copy.wait_recv()
    swap_other = project(1 - c)
    keep_x = pltpu.make_async_copy(rows_v, x_out, load_sem.at[7])
    keep_x.start()
    for n in (0, 128, 256):
        w_t[n : n + 128] = jnp.transpose(w_v[:, n : n + 128])
    swap_other.wait_recv()
    activate(1 - c)
    to_core = []
    for xx in (1 - x, x):
        src = res.at[pl.ds((1 - c) * 8 + xx * 4, 4)]
        to_core.append(remote(src, ra.at[pl.ds(xx * 4, 4)], peer_c))
    swap_own.wait_recv()
    activate(c)
    keep_act = pltpu.make_async_copy(act_v, act_out, load_sem.at[8])
    keep_act.start()
    to_core[0].wait_recv()
    to_x = [None] * 4
    for k in (3, 2, 1, 0):
        zz = near[k]
        sb[k] = (res[pos(zz, 1 - x, c)].astype(F32) + ra[(1 - x) * 4 + zz].astype(F32)).astype(BF16)
        to_x[k] = remote(sb.at[k], rb.at[k], peer_x)
    to_core[1].wait_recv()

    def summed(k):
        zz = near[k]
        mid = res[pos(zz, x, c)].astype(F32) + ra[x * 4 + zz].astype(F32)
        to_x[k].wait_recv()
        mid = mid + rb[k].astype(F32)
        out8, grad8 = mid[:8], mid[8:]
        for_0 = jnp.where(low, out8, pltpu.roll(grad8, 4, 0))
        for_1 = jnp.where(low, pltpu.roll(out8, 4, 0), grad8)
        return jnp.where(y == 0, for_0, for_1), jnp.where(y == 0, for_1, for_0)

    to_z = []
    for k in (3, 2, 1, 0):
        same, other = summed(k)
        sc[1, k] = fold(other).astype(BF16)
        to_z.append((1, k, remote(sc.at[1, k], rc.at[1, k], line[1][k])))
        if k:
            sc[0, k] = fold(same).astype(BF16)
            to_z.append((0, k, remote(sc.at[0, k], rc.at[0, k], line[0][k])))
    total = [same, jnp.zeros_like(same)]
    for s_y, k, copy in to_z:
        copy.wait_recv()
        total[s_y] = total[s_y] + unfold(rc[s_y, k].astype(F32))
    mine8, got8 = (t.astype(BF16).astype(F32) for t in total)
    scale = jnp.where(row_ids((8, 1)) < 4, gate8, 1.0)
    slot_out[:, :half] = jnp.where(y == 0, mine8, got8) * scale
    slot_out[:, half:] = jnp.where(y == 0, got8, mine8) * scale
    keep_x.wait()
    keep_act.wait()
    for copy in started:
        copy.wait_send()


def output_kernel(x_ref, act_ref, slot_ref, sel_ref, out_ref, tg_ref, gg_ref, gu_ref, gd_ref):
    sel = sel_ref[...]
    low = row_ids(sel.shape) < 4
    slots = slot_ref[...].astype(BF16)
    tn = (((0,), (0,)), ((), ()))
    for ref, keep in ((out_ref, low), (tg_ref, jnp.logical_not(low))):
        picks = jnp.where(keep, sel, 0.0).astype(BF16)
        ref[...] = lax.dot_general(picks, slots, tn, preferred_element_type=F32).astype(BF16)
    grads = lax.dot_general(x_ref[...], act_ref[...], tn, preferred_element_type=F32)
    for n, ref in enumerate((gg_ref, gu_ref, gd_ref)):
        ref[...] = grads[:, n * 128 : (n + 1) * 128]


def per_device_fused(tokens, out_cotangent, expert_ids, gate_fixed, w_gate, w_up, w_down):
    n_tok, width = tokens.shape
    half = width // 2
    hbm = pl.BlockSpec(memory_space=pltpu.HBM)
    vmem = pl.BlockSpec(memory_space=pltpu.VMEM)
    copies = 35
    chunks = lambda n: pltpu.VMEM((n, 16, half), BF16)
    pieces = lambda m, n: pltpu.VMEM((m, n, 16, half // 2), BF16)
    x_all, act, slots, sel = pl.pallas_call(
        exchange_kernel,
        out_shape=(
            pltpu.VMEM((16, 16, half), BF16),
            pltpu.VMEM((16, 16, 384), BF16),
            pltpu.VMEM((8, width), F32),
            pltpu.VMEM((8, n_tok), F32),
        ),
        in_specs=[hbm] * 7,
        out_specs=(vmem,) * 4,
        scratch_shapes=[
            pltpu.VMEM(expert_ids.shape[::-1], jnp.int32),
            pltpu.VMEM(gate_fixed.shape[::-1], jnp.int32),
            pltpu.VMEM((2 * n_tok, width), BF16),
            pltpu.VMEM((half, 384), BF16),
            pltpu.VMEM((384, half), BF16),
            pieces(16, 2),
            chunks(16),
            pltpu.VMEM((16, 16, 384), BF16),
            pltpu.VMEM((2, 64, 384), F32),
            pltpu.VMEM((2, 64, 384), BF16),
            pltpu.VMEM((2, 64, 384), BF16),
            chunks(16),
            chunks(8),
            chunks(4),
            chunks(4),
            pieces(2, 4),
            pieces(2, 4),
            pltpu.VMEM((16, half // 2), BF16),
            pltpu.SemaphoreType.DMA((9,)),
            pltpu.SemaphoreType.DMA((copies,)),
            pltpu.SemaphoreType.DMA((copies,)),
        ],
        compiler_params=pltpu.CompilerParams(
            collective_id=0, has_side_effects=True, vmem_limit_bytes=60 * 1024 * 1024
        ),
        cost_estimate=pl.CostEstimate(flops=400_000_000, bytes_accessed=6_000_000, transcendentals=16384),
        name="exchange",
    )(expert_ids.T, gate_fixed.T, tokens, out_cotangent, w_gate[0], w_up[0], w_down[0])
    steps = 2
    grad_spec = pl.BlockSpec((half // steps, 128), lambda i: (i, 0))
    tok_spec = pl.BlockSpec((n_tok, width // steps), lambda i: (0, i))
    layer_out, token_grad, gg, gu, gd = pl.pallas_call(
        output_kernel,
        grid=(steps,),
        out_shape=(jax.ShapeDtypeStruct((n_tok, width), BF16),) * 2
        + (jax.ShapeDtypeStruct((half, 128), F32),) * 3,
        in_specs=[
            pl.BlockSpec((256, half // steps), lambda i: (0, i)),
            pl.BlockSpec((256, 384), lambda i: (0, 0)),
            pl.BlockSpec((8, width // steps), lambda i: (0, i)),
            pl.BlockSpec((8, n_tok), lambda i: (0, 0)),
        ],
        out_specs=(tok_spec, tok_spec, grad_spec, grad_spec, grad_spec),
        compiler_params=pltpu.CompilerParams(vmem_limit_bytes=32 * 1024 * 1024),
        cost_estimate=pl.CostEstimate(flops=400_000_000, bytes_accessed=6_000_000, transcendentals=0),
        name="outputs",
    )(x_all.reshape(256, half), act.reshape(256, 384), slots, sel)
    return (layer_out, token_grad, gg[None], gu[None], gd[None])


def solution(mesh):
    sizes = (mesh.shape["dp"], mesh.shape["expert"])
    return jax.shard_map(
        per_device_fused if sizes == (2, 16) else per_device,
        mesh=mesh,
        in_specs=(
            P(("dp", "expert"), None),
            P(("dp", "expert"), None),
            P(("dp", "expert"), None),
            P(("dp", "expert"), None),
            P("expert", "dp", None),
            P("expert", "dp", None),
            P("expert", "dp", None),
        ),
        out_specs=(
            P(("dp", "expert"), None),
            P(("dp", "expert"), None),
            P("expert", "dp", None),
            P("expert", "dp", None),
            P("expert", "dp", None),
        ),
        check_vma=False,
    )
```
